256 devices in a mesh: slab: 32 (over z_lo, y, core), head: 8 (over z_hi, x).
Axes of the slice: x: 4, y: 4, z: 8 (z_hi: 2, z_lo: 4; z = z_hi * 4 + z_lo), core: 2. Of those that a mesh axis runs over, the one named last changes fastest.
Arguments:
- queries: bfloat16 [4096, 3072], P('slab', 'head'), may hold values from -20 to 20
- keys: bfloat16 [4096, 3072], P('slab', 'head'), may hold values from -20 to 20
- values: bfloat16 [4096, 3072], P('slab', 'head'), may hold values from -6 to 6
- w_out: bfloat16 [3072, 3072], P('head'), may hold values from -0.109375 to 0.109375
- d_out: bfloat16 [4096, 3072], P('slab', 'head'), may hold values from -6 to 6
- far_ids: int32 [64, 4], P('slab'), may hold values from 0 to 63, as said below
- far_counts: int32 [64], P('slab'), may hold values from 0 to 4, as said below
Outputs:
- mixed: bfloat16 [4096, 3072], P('slab', 'head')
- query_grad: bfloat16 [4096, 3072], P('slab', 'head')
- key_grad: bfloat16 [4096, 3072], P('slab', 'head')
- value_grad: bfloat16 [4096, 3072], P('slab', 'head')
- weight_grad: float32 [3072, 3072], P(('head', 'slab'))
The draws below stay inside these ranges and needn't reach their ends.
Inputs may be any that keep to these rules, and one draw needn't show every extreme that they name: `far_ids`: within each aligned block of 2 rows, the 8 values id // 2 are all different. `far_counts`: each aligned block of 2 entries holds 4 at least once.
All inputs are finite; a program needn't handle non-finite values.
Results may differ from the reference program's by a relative error of at most 0.028.
Values may be sent and summed in bfloat16 or wider, within the bound.
No kernel may reach another device: no remote copies, remote signals or barrier semaphores. Data moves between devices by JAX's collectives and lax.ppermute only.
A program may use at most 192 MiB of HBM per device.

```python
import math
import jax
import jax.numpy as jnp
import numpy as np
from jax import lax

D = 3072
HEADS = 24
HD = 128
TILE = 64
TT_DEV = 1
TH_DEV = 1
SLAB_H = 8
TW = 2
FAR = 4
TILES_DEV = 2
TILES_ALL = 64
TOKENS = 4096
TIME_TILES = 4
HEIGHT_TILES = 8


def drawn_rows(key, salt):
    return jnp.clip(jax.random.normal(jax.random.fold_in(key, salt), (TOKENS, D), jnp.float32), -6.0, 6.0)


def draw_queries(key, part):
    base = drawn_rows(key, 1)
    return base.astype(jnp.bfloat16)


def draw_keys(key, part):
    base = drawn_rows(key, 2)
    return base.astype(jnp.bfloat16)


def draw_far_ids(key, part):
    slab_count = TILES_ALL // TILES_DEV
    split_keys = jax.random.split(jax.random.fold_in(key, 21), slab_count)

    def owners_of(one_key):
        return jax.random.permutation(one_key, slab_count)[:TILES_DEV * FAR]
    owners = jax.vmap(owners_of)(split_keys).astype(jnp.int32)
    local = jax.random.randint(jax.random.fold_in(key, 22), (slab_count, TILES_DEV * FAR), 0, TILES_DEV, dtype=jnp.int32)
    return (owners * TILES_DEV + local).reshape(TILES_ALL, FAR).astype(jnp.int32)


def draw_far_counts(key, part):
    slab_count = TILES_ALL // TILES_DEV
    counts = jax.random.randint(jax.random.fold_in(key, 31), (slab_count, TILES_DEV), 0, FAR + 1, dtype=jnp.int32)
    chosen = jax.random.randint(jax.random.fold_in(key, 32), (slab_count, 1), 0, TILES_DEV, dtype=jnp.int32)
    counts = jnp.where(jnp.arange(TILES_DEV, dtype=jnp.int32)[None, :] == chosen, FAR, counts)
    return counts.reshape(TILES_ALL).astype(jnp.int32)


def shard_levels(stream_key, extent, shards, low, largest):
    level, own = 1.0, jax.random.fold_in(stream_key, 6)
    for position, parts in shards:
        draws = jnp.exp(jax.random.uniform(jax.random.fold_in(own, position), (parts,), jnp.float32, low / len(shards), largest / len(shards)))
        level = level * jnp.repeat(draws, extent[position] // parts).reshape([-1 if axis == position else 1 for axis in range(len(extent))])
    return level


def scatter_about(own_key, extent, width, limit, cuts=(), held_as=jnp.bfloat16):
    entries = width * jax.random.normal(own_key, extent, jnp.float32)
    if cuts:
        entries = entries * shard_levels(own_key, extent, cuts, -0.22, 0.18)
    return jnp.clip(entries, -limit, limit).astype(held_as)


def setup_inputs(seed: int = 0) -> dict:
    splits = jax.random.split(jax.random.key(seed), 8)
    queries = draw_queries(jax.random.fold_in(splits[7], 71), 0)
    keys = draw_keys(jax.random.fold_in(splits[7], 71), 0)
    values = scatter_about(splits[2], (TOKENS, D), 1.0, 6.0, ((0, 32), (1, 8)))
    w_out = scatter_about(splits[3], (D, D), D ** -0.5, 0.109375, ((0, 8),))
    d_out = scatter_about(splits[4], (TOKENS, D), 1.0, 6.0, ((0, 32), (1, 8)))
    far_ids = draw_far_ids(jax.random.fold_in(splits[7], 71), 0)
    far_counts = draw_far_counts(jax.random.fold_in(splits[7], 71), 0)
    return dict(queries=queries, keys=keys, values=values, w_out=w_out, d_out=d_out, far_ids=far_ids, far_counts=far_counts)


NEIGHBOURS = np.array([[first, second, third] for first in (-1, 0, 1) for second in (-1, 0, 1) for third in (-1, 0, 1)], dtype=np.int32)
NEG_FILL = -1e+30

def tile_place(tile_index):
    slab_index = tile_index // TILES_DEV
    local_index = tile_index % TILES_DEV
    time_coord = slab_index // SLAB_H * TT_DEV + local_index // (TH_DEV * TW)
    height_coord = slab_index % SLAB_H * TH_DEV + local_index // TW % TH_DEV
    width_coord = local_index % TW
    return (time_coord, height_coord, width_coord)

def tile_number(time_coord, height_coord, width_coord):
    slab_index = time_coord // TT_DEV * SLAB_H + height_coord // TH_DEV
    local_index = (time_coord % TT_DEV * TH_DEV + height_coord % TH_DEV) * TW + width_coord
    return slab_index * TILES_DEV + local_index

def key_sets(far_ids, far_counts):
    tile_index = jnp.arange(TILES_ALL, dtype=jnp.int32)
    time_coord, height_coord, width_coord = tile_place(tile_index)
    offsets = jnp.asarray(NEIGHBOURS, dtype=jnp.int32)
    time_near = time_coord[:, None] + offsets[None, :, 0]
    height_near = height_coord[:, None] + offsets[None, :, 1]
    width_near = width_coord[:, None] + offsets[None, :, 2]
    inside = (time_near >= 0) & (time_near < TIME_TILES) & (height_near >= 0) & (height_near < HEIGHT_TILES) & (width_near >= 0) & (width_near < TW)
    near_ids = tile_number(jnp.clip(time_near, 0, TIME_TILES - 1), jnp.clip(height_near, 0, HEIGHT_TILES - 1), jnp.clip(width_near, 0, TW - 1))
    far_live = jnp.arange(FAR, dtype=jnp.int32)[None, :] < far_counts[:, None]
    key_ids = jnp.concatenate([near_ids.astype(jnp.int32), far_ids.astype(jnp.int32)], axis=1)
    return (key_ids, jnp.concatenate([inside, far_live], axis=1))

def reference(queries, keys, values, w_out, d_out, far_ids, far_counts):
    score_scale = 1.0 / math.sqrt(HD)
    query_tiles = queries.reshape(TILES_ALL, TILE, HEADS, HD)
    key_tiles = keys.reshape(TILES_ALL, TILE, HEADS, HD)
    value_tiles = values.reshape(TILES_ALL, TILE, HEADS, HD)
    key_ids, key_live = key_sets(far_ids, far_counts)
    key_count = key_ids.shape[1]

    def gather_rows(table, tile_ids):
        return table[tile_ids].reshape(key_count * TILE, HEADS, HD).astype(jnp.float32)

    def masked_scores(query_tile, tile_ids, live):
        scores = jnp.einsum('thd,khd->htk', query_tile.astype(jnp.float32), gather_rows(key_tiles, tile_ids)) * score_scale
        key_mask = jnp.repeat(live, TILE)[None, None, :]
        return (jnp.where(key_mask, scores, NEG_FILL), key_mask)

    def forward_tile(inputs):
        query_tile, tile_ids, live = inputs
        scores, key_mask = masked_scores(query_tile, tile_ids, live)
        maximum = lax.optimization_barrier(jnp.max(scores, axis=-1, keepdims=True))
        exp_terms = jnp.where(key_mask, jnp.exp(scores - maximum), 0.0)
        row_total = lax.optimization_barrier(jnp.sum(exp_terms, axis=-1, keepdims=True))
        weights = lax.optimization_barrier((exp_terms / row_total).astype(jnp.bfloat16)).astype(jnp.float32)
        attended = jnp.einsum('htk,khd->thd', weights, gather_rows(value_tiles, tile_ids))
        return (attended.astype(jnp.bfloat16), (maximum + jnp.log(row_total))[:, :, 0])
    attended, log_total = lax.map(forward_tile, (query_tiles, key_ids, key_live))
    attended_flat = attended.reshape(TOKENS, D)
    mixed = jnp.dot(attended_flat, w_out, preferred_element_type=jnp.float32).astype(jnp.bfloat16)
    grad_attended = jnp.dot(d_out, w_out.T, preferred_element_type=jnp.float32).astype(jnp.bfloat16)
    weight_grad = jnp.dot(attended_flat.T, d_out, preferred_element_type=jnp.float32)
    grad_tiles = grad_attended.reshape(TILES_ALL, TILE, HEADS, HD)
    row_delta = lax.optimization_barrier(jnp.sum(grad_tiles.astype(jnp.float32) * attended.astype(jnp.float32), axis=-1)).transpose(0, 2, 1)

    def backward_tile(carry, inputs):
        key_grad, value_grad = carry
        query_tile, grad_tile, log_tile, delta_tile, tile_ids, live = inputs
        scores, key_mask = masked_scores(query_tile, tile_ids, live)
        back_weights = jnp.where(key_mask, jnp.exp(scores - log_tile[:, :, None]), 0.0)
        back_low = lax.optimization_barrier(back_weights.astype(jnp.bfloat16)).astype(jnp.float32)
        grad_float = grad_tile.astype(jnp.float32)
        value_part = jnp.einsum('htk,thd->khd', back_low, grad_float)
        grad_weights = jnp.einsum('thd,khd->htk', grad_float, gather_rows(value_tiles, tile_ids))
        grad_scores = lax.optimization_barrier((back_weights * (grad_weights - delta_tile[:, :, None])).astype(jnp.bfloat16)).astype(jnp.float32)
        query_part = jnp.einsum('htk,khd->thd', grad_scores, gather_rows(key_tiles, tile_ids)) * score_scale
        key_part = jnp.einsum('htk,thd->khd', grad_scores, query_tile.astype(jnp.float32)) * score_scale
        key_grad = key_grad.at[tile_ids].add(key_part.reshape(key_count, TILE, HEADS, HD))
        value_grad = value_grad.at[tile_ids].add(value_part.reshape(key_count, TILE, HEADS, HD))
        return ((key_grad, value_grad), query_part.astype(jnp.bfloat16))
    empty = jnp.zeros((TILES_ALL, TILE, HEADS, HD), jnp.float32)
    (key_grad, value_grad), query_grad = lax.scan(backward_tile, (empty, empty), (query_tiles, grad_tiles, log_total, row_delta, key_ids, key_live))
    return (mixed, query_grad.reshape(TOKENS, D), key_grad.reshape(TOKENS, D).astype(jnp.bfloat16), value_grad.reshape(TOKENS, D).astype(jnp.bfloat16), weight_grad)
```

```python
import functools
import math

import jax
import jax.numpy as jnp
from jax import lax
from jax.experimental import pallas as pl
from jax.experimental.pallas import tpu as pltpu
from jax.sharding import PartitionSpec as P

HD = 128
TILE = 64
HEADS = 3
ROWS = 128
COLS = 384
WIDE = 3072
NT_DEV = 4
NY_DEV = 4
DEAD = -1e30
SCALE = 1.0 / math.sqrt(HD)
BF = jnp.bfloat16
F32 = jnp.float32


def swap(block, axis, distance):
    devices = range(lax.axis_size(axis))
    return lax.ppermute(block, axis, [(i, i ^ distance) for i in devices])


def dot(lhs, rhs, left, right):
    return lax.dot_general(lhs, rhs, (((left,), (right,)), ((), ())), preferred_element_type=F32)


def call(kernel, outs, *args, flops, moved, scratch=()):
    vmem = pl.BlockSpec(memory_space=pltpu.VMEM)
    smem = pl.BlockSpec(memory_space=pltpu.SMEM)
    return pl.pallas_call(
        kernel,
        out_shape=[jax.ShapeDtypeStruct(shape, dtype) for shape, dtype in outs],
        in_specs=[smem if a.dtype == jnp.int32 else vmem for a in args],
        out_specs=[vmem] * len(outs),
        scratch_shapes=list(scratch),
        compiler_params=pltpu.CompilerParams(vmem_limit_bytes=40 * 1024 * 1024),
        cost_estimate=pl.CostEstimate(flops=flops, bytes_accessed=moved, transcendentals=0),
    )(*args)


def forward_kernel(*refs):
    q_refs, kv_refs, bias_ref = refs[:4], refs[4:12], refs[12]
    out_refs, s_ref = refs[13:17], refs[17]
    row = lax.broadcasted_iota(jnp.int32, (16, 4 * ROWS), 0)
    stats = jnp.zeros((16, 4 * ROWS), F32)
    for h in range(HEADS):
        cols = slice(h * HD, (h + 1) * HD)
        q = jnp.concatenate([r[:, cols] for r in q_refs], axis=0)
        top = jnp.full((1, 4 * ROWS), 2 * DEAD, F32)
        for b, kv in enumerate(kv_refs):
            s = dot(kv[0:ROWS, cols], q, 1, 1) * SCALE
            for half in range(2):
                part = s[half * TILE : (half + 1) * TILE] + bias_ref[2 * b + half : 2 * b + half + 1, :]
                start = b * ROWS + half * TILE
                s_ref[start : start + TILE, :] = part
                top = jnp.maximum(top, jnp.max(part, axis=0, keepdims=True))
        total = jnp.zeros((1, 4 * ROWS), F32)
        out = jnp.zeros((HD, 4 * ROWS), F32)
        for b, kv in enumerate(kv_refs):
            e = jnp.exp(s_ref[b * ROWS : (b + 1) * ROWS, :] - top)
            total = total + jnp.sum(e, axis=0, keepdims=True)
            out = out + dot(kv[ROWS : 2 * ROWS, cols], e.astype(BF), 0, 0)
        out = (out / total).astype(BF)
        for j, r in enumerate(out_refs):
            r[cols, :] = out[:, j * ROWS : (j + 1) * ROWS]
        rest = top + jnp.log(total)
        for piece in range(3):
            high = rest.astype(BF).astype(F32)
            stats = jnp.where(row == 3 * h + piece, high, stats)
            rest = rest - high
    stats = stats.astype(BF)
    for j, r in enumerate(out_refs):
        r[COLS : COLS + 16, :] = stats[:, j * ROWS : (j + 1) * ROWS]


def merge_kernel(*refs):
    parts, grad_ref, att_ref, stats_ref = refs[:4], refs[4], refs[5], refs[6]
    row = lax.broadcasted_iota(jnp.int32, (8, ROWS), 0)
    stats = jnp.zeros((8, ROWS), F32)
    pieces = [r[COLS : COLS + 16, :].astype(F32) for r in parts]
    for h in range(HEADS):
        cols = slice(h * HD, (h + 1) * HD)
        logs = [(p[3 * h : 3 * h + 1] + p[3 * h + 1 : 3 * h + 2]) + p[3 * h + 2 : 3 * h + 3] for p in pieces]
        top = functools.reduce(jnp.maximum, logs)
        shares = [jnp.exp(l - top) for l in logs]
        total = functools.reduce(jnp.add, shares)
        out = sum((r[cols, :].astype(F32) * (w / total) for r, w in zip(parts, shares)), jnp.zeros((HD, ROWS), F32))
        out = out.astype(BF)
        att_ref[cols, :] = out
        delta = jnp.sum(out.astype(F32) * grad_ref[cols, :].astype(F32), axis=0, keepdims=True)
        stats = jnp.where(row == h, top + jnp.log(total), stats)
        stats = jnp.where(row == 3 + h, delta, stats)
    stats_ref[...] = stats


def grad_kernel(rank_ref, w_ref, d_ref, out_ref):
    total = jnp.zeros((COLS, ROWS), F32)
    for p in range(8):
        start = pl.multiple_of((rank_ref[3] ^ p) * COLS, 128)
        total = total + dot(w_ref[:, pl.ds(start, COLS)], d_ref[p * ROWS : (p + 1) * ROWS, :], 1, 1)
    out_ref[...] = total.astype(BF)


def mix_kernel(rank_ref, att_ref, w_ref, own_ref, *out_refs):
    att = att_ref[...].T
    for j in range(4):
        for k in range(2):
            start = pl.multiple_of((rank_ref[3] ^ (4 * k + j)) * COLS, 128)
            part = jnp.dot(att, w_ref[:, pl.ds(start, COLS)], preferred_element_type=F32)
            rows = slice(k * ROWS, (k + 1) * ROWS)
            if j == 0:
                own_ref[rows, :] = part
            else:
                out_refs[j - 1][rows, :] = part.astype(BF)


def weight_kernel(rank_ref, att_ref, att2_ref, d_ref, d2_ref, own_ref, *out_refs):
    t, y, c = rank_ref[0], rank_ref[1], rank_ref[2]
    row = lax.broadcasted_iota(jnp.int32, (192, COLS), 0)
    col = lax.broadcasted_iota(jnp.int32, (192, COLS), 1)
    source = row * 0
    for jy in range(4):
        for jt in range(4):
            low = jy * 48 + jt * 12
            base = (t ^ jt) * 96 + (y ^ jy) * 24 + c * 12 - low
            source = jnp.where((row >= low) & (row < low + 12), row + base, source)
    pick = jnp.where(source == col, 1.0, 0.0).astype(BF)
    first = jnp.dot(pick, att_ref[...], preferred_element_type=F32).astype(BF)
    second = jnp.dot(pick, att2_ref[...], preferred_element_type=F32).astype(BF)
    both = jnp.concatenate([first, second], axis=1)
    for p in range(8):
        start = pl.multiple_of((rank_ref[3] ^ p) * COLS, 128)
        rows = slice(p * ROWS, (p + 1) * ROWS)
        rhs = jnp.concatenate([d_ref[rows, :], d2_ref[rows, :]], axis=0)
        part = jnp.dot(both, rhs, preferred_element_type=F32)
        own_ref[:, pl.ds(start, COLS)] = part[0:48]
        for j in range(3):
            out_refs[j][:, pl.ds(start, COLS)] = part[48 * (j + 1) : 48 * (j + 2)].astype(BF)


def backward_kernel(*refs):
    q_refs, kv_refs, bias_ref = refs[:4], refs[4:12], refs[12]
    g_refs, stat_refs = refs[13:17], refs[17:21]
    dq_refs, own_ref, other_ref = refs[21:25], refs[25], refs[26]
    for h in range(HEADS):
        cols = slice(h * HD, (h + 1) * HD)
        q = jnp.concatenate([r[:, cols] for r in q_refs], axis=0)
        g = jnp.concatenate([r[cols, :] for r in g_refs], axis=1)
        log_total = jnp.concatenate([r[h : h + 1, :] for r in stat_refs], axis=1)
        delta = jnp.concatenate([r[3 + h : 4 + h, :] for r in stat_refs], axis=1)
        dq = jnp.zeros((HD, 4 * ROWS), F32)
        for b, kv in enumerate(kv_refs):
            k, v = kv[0:ROWS, cols], kv[ROWS : 2 * ROWS, cols]
            s = dot(k, q, 1, 1) * SCALE
            bias = [
                jnp.broadcast_to(bias_ref[2 * b + half : 2 * b + half + 1, :], (TILE, 4 * ROWS)) for half in range(2)
            ]
            p = jnp.exp(s + jnp.concatenate(bias, axis=0) - log_total)
            ds = (p * (jnp.dot(v, g, preferred_element_type=F32) - delta)).astype(BF)
            dv = dot(p.astype(BF), g, 1, 1)
            dk = jnp.dot(ds, q, preferred_element_type=F32) * SCALE
            dq = dq + dot(k, ds, 0, 0)
            place = (b % 4) * 2 * ROWS
            target = own_ref if b < 4 else other_ref
            target[place : place + ROWS, cols] = dk.astype(target.dtype)
            target[place + ROWS : place + 2 * ROWS, cols] = dv.astype(target.dtype)
        dq = (dq * SCALE).astype(BF)
        for j, r in enumerate(dq_refs):
            r[cols, :] = dq[:, j * ROWS : (j + 1) * ROWS]


def on_device(queries, keys, values, w_out, d_out, far_ids, far_counts):
    slab = lax.axis_index("slab")
    head = lax.axis_index("head")
    t, y, c = slab // 8, slab // 2 % 4, slab % 2
    ranks = jnp.stack([t, y, c, head]).astype(jnp.int32)

    kv = jnp.concatenate([keys, values], axis=0)
    kv_near = [kv] + [swap(kv, "slab", 2 * e) for e in (1, 2, 3)]
    named = jnp.where(jnp.arange(4, dtype=jnp.int32)[None, :] < far_counts[:, None], far_ids, -1)
    named = [named] + [swap(named, "slab", 8 * j) for j in (1, 2, 3)]
    q_all = [queries] + [swap(queries, "slab", 8 * j) for j in (1, 2, 3)]
    kv_far = [swap(block, "slab", 1) for block in kv_near]
    kv_all = kv_near + kv_far

    d_blocks = [d_out] + [swap(d_out, "head", j) for j in (1, 2, 3)]
    d_across = swap(d_out, "head", 4)
    d_blocks += [d_across] + [swap(d_across, "head", j) for j in (1, 2, 3)]
    d_full = jnp.concatenate(d_blocks, axis=0)
    d_other = swap(d_full, "slab", 1)

    step = jnp.arange(4, dtype=jnp.int32)
    key_height = jnp.concatenate([(y ^ step) * 2 + c, (y ^ step) * 2 + (1 - c)])
    key_tile = ((t * 8 + key_height)[:, None] * 2 + jnp.arange(2, dtype=jnp.int32)[None, :]).reshape(16)
    near_time = jnp.abs((t ^ step) - t) <= 1
    near_height = jnp.abs(key_height - (y * 2 + c)) <= 1
    near = (jnp.repeat(near_height, 2)[:, None] & jnp.repeat(near_time, 2)[None, :]).astype(F32)
    named_all = jnp.concatenate(named, axis=0)
    count = near + jnp.sum((named_all[None] == key_tile[:, None, None]).astype(F32), axis=-1)
    bias = jnp.where(count > 0, jnp.log(jnp.maximum(count, 1.0)), DEAD)
    bias = jnp.repeat(bias, TILE, axis=1)

    grad = call(grad_kernel, [((COLS, ROWS), BF)], ranks, w_out, d_full, flops=3 * 10**8, moved=3 * 10**6)[0]
    g_all = [grad] + [swap(grad, "slab", 8 * j) for j in (1, 2, 3)]

    parts = call(
        forward_kernel,
        [((COLS + 16, ROWS), BF)] * 4,
        *q_all,
        *kv_all,
        bias,
        flops=3 * 10**9,
        moved=3 * 10**6,
        scratch=[pltpu.VMEM((8 * ROWS, 4 * ROWS), F32)],
    )
    parts = [parts[0]] + [swap(parts[j], "slab", 8 * j) for j in (1, 2, 3)]
    att, stats = call(
        merge_kernel, [((COLS, ROWS), BF), ((8, ROWS), F32)], *parts, grad, flops=10**8, moved=10**6
    )
    stat_all = [stats] + [swap(stats, "slab", 8 * j) for j in (1, 2, 3)]
    att_other = swap(att, "slab", 1)

    mix = call(
        mix_kernel,
        [((2 * ROWS, COLS), F32)] + [((2 * ROWS, COLS), BF)] * 3,
        ranks,
        att,
        w_out,
        flops=3 * 10**8,
        moved=4 * 10**6,
    )
    mixed_pair = mix[0] + sum((swap(mix[j], "head", j).astype(F32) for j in (1, 2, 3)), 0.0)
    mixed = mixed_pair[:ROWS] + swap(mixed_pair[ROWS:].astype(BF), "head", 4).astype(F32)

    weight = call(
        weight_kernel,
        [((48, WIDE), F32)] + [((48, WIDE), BF)] * 3,
        ranks,
        att,
        att_other,
        d_full,
        d_other,
        flops=6 * 10**8,
        moved=4 * 10**6,
    )
    weight = weight[0] + sum((swap(weight[j], "slab", 2 * j).astype(F32) for j in (1, 2, 3)), 0.0)
    weight_grad = weight[:12] + sum(
        (swap(weight[12 * j : 12 * (j + 1)].astype(BF), "slab", 8 * j).astype(F32) for j in (1, 2, 3)), 0.0
    )

    back = call(
        backward_kernel,
        [((COLS, ROWS), BF)] * 4 + [((8 * ROWS, COLS), F32), ((8 * ROWS, COLS), BF)],
        *q_all,
        *kv_all,
        bias,
        *g_all,
        *stat_all,
        flops=6 * 10**9,
        moved=6 * 10**6,
    )
    dq = back[0].astype(F32) + sum((swap(back[j], "slab", 8 * j).astype(F32) for j in (1, 2, 3)), 0.0)
    query_grad = dq.astype(BF).T
    pair = (back[4] + swap(back[5], "slab", 1).astype(F32)).reshape(4, 2 * ROWS, COLS)
    total = pair[0] + sum((swap(pair[e].astype(BF), "slab", 2 * e).astype(F32) for e in (1, 2, 3)), 0.0)
    total = total.astype(BF)
    return mixed.astype(BF), query_grad, total[:ROWS], total[ROWS:], weight_grad


def solution(mesh):
    placed = (
        P("slab", "head"),
        P("slab", "head"),
        P("slab", "head"),
        P("head", None),
        P("slab", "head"),
        P("slab", None),
        P("slab"),
    )
    return jax.shard_map(
        on_device,
        mesh=mesh,
        in_specs=placed,
        out_specs=(
            P("slab", "head"),
            P("slab", "head"),
            P("slab", "head"),
            P("slab", "head"),
            P(("head", "slab"), None),
        ),
        check_vma=False,
    )
```

```python
import functools
import math

import jax
import jax.numpy as jnp
from jax import lax
from jax.experimental import pallas as pl
from jax.experimental.pallas import tpu as pltpu
from jax.sharding import PartitionSpec as P

HD = 128
TILE = 64
HEADS = 3
ROWS = 128
COLS = 384
WIDE = 3072
NT_DEV = 4
NY_DEV = 4
DEAD = -1e30
SCALE = 1.0 / math.sqrt(HD)
ORDER = (0, 4, 1, 5, 2, 6, 3, 7)
BF = jnp.bfloat16
F32 = jnp.float32


def swap(block, axis, distance):
    devices = range(lax.axis_size(axis))
    return lax.ppermute(block, axis, [(i, i ^ distance) for i in devices])


def gathered(block, axis, unit):
    near = swap(block, axis, unit)
    rows = block.shape[0]
    far = swap(jnp.concatenate([block, near], axis=0), axis, 2 * unit)
    return [block, near, far[:rows], far[rows:]]


def dot(lhs, rhs, left, right):
    return lax.dot_general(lhs, rhs, (((left,), (right,)), ((), ())), preferred_element_type=F32)


def call(kernel, outs, *args, flops, moved, scratch=()):
    vmem = pl.BlockSpec(memory_space=pltpu.VMEM)
    smem = pl.BlockSpec(memory_space=pltpu.SMEM)
    return pl.pallas_call(
        kernel,
        out_shape=[jax.ShapeDtypeStruct(shape, dtype) for shape, dtype in outs],
        in_specs=[smem if a.dtype == jnp.int32 else vmem for a in args],
        out_specs=[vmem] * len(outs),
        scratch_shapes=list(scratch),
        compiler_params=pltpu.CompilerParams(vmem_limit_bytes=40 * 1024 * 1024),
        cost_estimate=pl.CostEstimate(flops=flops, bytes_accessed=moved, transcendentals=0),
    )(*args)


def pack_kernel(ids_ref, counts_ref, q_ref, k_ref, v_ref, q_out, kv_out):
    q_out[0:ROWS, :] = q_ref[...]
    row = lax.broadcasted_iota(jnp.int32, (16, COLS), 0)
    col = lax.broadcasted_iota(jnp.int32, (16, COLS), 1)
    named = jnp.full((16, COLS), -1.0, F32)
    for tile in range(2):
        for f in range(4):
            one = jnp.where(f < counts_ref[tile], ids_ref[tile, f], -1).astype(F32)
            named = jnp.where((row == tile) & (col == f), one, named)
    q_out[ROWS : ROWS + 16, :] = named.astype(BF)
    kv_out[0:ROWS, :] = k_ref[...]
    kv_out[ROWS : 2 * ROWS, :] = v_ref[...]


def log_counts(rank_ref, q_refs):
    t, y, c = rank_ref[0], rank_ref[1], rank_ref[2]
    row = lax.broadcasted_iota(jnp.int32, (16, ROWS), 0)
    lane = lax.broadcasted_iota(jnp.int32, (16, ROWS), 1)
    block = row // 2
    height = (y ^ (block % 4)) * 2 + (c ^ (block // 4))
    tile = (((t * 8 + height) * 2) + row % 2).astype(F32)
    near_height = jnp.abs(height - (y * 2 + c)) <= 1
    parts = []
    for j, q in enumerate(q_refs):
        near_time = jnp.abs((t ^ j) - t) <= 1
        count = jnp.where(near_height & near_time, 1.0, 0.0)
        named = q[ROWS : ROWS + 16, 0:HD].astype(F32)
        for f in range(4):
            one = jnp.where(lane < TILE, named[0:1, f : f + 1], named[1:2, f : f + 1])
            count = count + jnp.where(one == tile, 1.0, 0.0)
        parts.append(jnp.where(count > 0, jnp.log(jnp.maximum(count, 1.0)), DEAD))
    return jnp.concatenate(parts, axis=1)


def forward_kernel(*refs):
    rank_ref, q_refs, kv_refs = refs[0], refs[1:5], refs[5:13]
    out_refs, s_ref, bias_ref = refs[13:17], refs[17], refs[18]
    bias_ref[...] = log_counts(rank_ref, q_refs)
    row = lax.broadcasted_iota(jnp.int32, (16, 4 * ROWS), 0)
    stats = jnp.zeros((16, 4 * ROWS), F32)
    for h in range(HEADS):
        cols = slice(h * HD, (h + 1) * HD)
        q = jnp.concatenate([r[0:ROWS, cols] for r in q_refs], axis=0)
        top = jnp.full((1, 4 * ROWS), 2 * DEAD, F32)
        for b, kv in enumerate(kv_refs):
            s = dot(kv[0:ROWS, cols], q, 1, 1) * SCALE
            for half in range(2):
                part = s[half * TILE : (half + 1) * TILE] + bias_ref[2 * b + half : 2 * b + half + 1, :]
                start = b * ROWS + half * TILE
                s_ref[start : start + TILE, :] = part
                top = jnp.maximum(top, jnp.max(part, axis=0, keepdims=True))
        total = jnp.zeros((1, 4 * ROWS), F32)
        out = jnp.zeros((HD, 4 * ROWS), F32)
        for b, kv in enumerate(kv_refs):
            e = jnp.exp(s_ref[b * ROWS : (b + 1) * ROWS, :] - top)
            total = total + jnp.sum(e, axis=0, keepdims=True)
            out = out + dot(kv[ROWS : 2 * ROWS, cols], e.astype(BF), 0, 0)
        out = (out / total).astype(BF)
        for j, r in enumerate(out_refs):
            r[cols, :] = out[:, j * ROWS : (j + 1) * ROWS]
        rest = top + jnp.log(total)
        for piece in range(3):
            high = rest.astype(BF).astype(F32)
            stats = jnp.where(row == 3 * h + piece, high, stats)
            rest = rest - high
    stats = stats.astype(BF)
    for j, r in enumerate(out_refs):
        r[COLS : COLS + 16, :] = stats[:, j * ROWS : (j + 1) * ROWS]


def merge_kernel(*refs):
    parts, grad_ref, att_ref, stats_ref = refs[:4], refs[4], refs[5], refs[6]
    row = lax.broadcasted_iota(jnp.int32, (8, ROWS), 0)
    stats = jnp.zeros((8, ROWS), F32)
    pieces = [r[COLS : COLS + 16, :].astype(F32) for r in parts]
    for h in range(HEADS):
        cols = slice(h * HD, (h + 1) * HD)
        logs = [(p[3 * h : 3 * h + 1] + p[3 * h + 1 : 3 * h + 2]) + p[3 * h + 2 : 3 * h + 3] for p in pieces]
        top = functools.reduce(jnp.maximum, logs)
        shares = [jnp.exp(l - top) for l in logs]
        total = functools.reduce(jnp.add, shares)
        out = sum((r[cols, :].astype(F32) * (w / total) for r, w in zip(parts, shares)), jnp.zeros((HD, ROWS), F32))
        out = out.astype(BF)
        att_ref[cols, :] = out
        delta = jnp.sum(out.astype(F32) * grad_ref[cols, :].astype(F32), axis=0, keepdims=True)
        stats = jnp.where(row == h, top + jnp.log(total), stats)
        stats = jnp.where(row == 3 + h, delta, stats)
    stats_ref[...] = stats


def grad_kernel(rank_ref, w_ref, d_ref, out_ref):
    total = jnp.zeros((COLS, ROWS), F32)
    for p in range(8):
        start = pl.multiple_of((rank_ref[3] ^ ORDER[p]) * COLS, 128)
        total = total + dot(w_ref[:, pl.ds(start, COLS)], d_ref[p * ROWS : (p + 1) * ROWS, :], 1, 1)
    out_ref[...] = total.astype(BF)


def mix_kernel(rank_ref, att_ref, w_ref, own_ref, other_ref):
    att = att_ref[...].T
    for i, p in enumerate(ORDER):
        start = pl.multiple_of((rank_ref[3] ^ p) * COLS, 128)
        part = jnp.dot(att, w_ref[:, pl.ds(start, COLS)], preferred_element_type=F32)
        target = own_ref if i < 4 else other_ref
        target[(i % 4) * ROWS : (i % 4 + 1) * ROWS, :] = part.astype(target.dtype)


def weight_kernel(rank_ref, att_ref, att2_ref, d_ref, d2_ref, own_ref, *out_refs):
    t, y, c = rank_ref[0], rank_ref[1], rank_ref[2]
    row = lax.broadcasted_iota(jnp.int32, (192, COLS), 0)
    col = lax.broadcasted_iota(jnp.int32, (192, COLS), 1)
    source = row * 0
    for jy in range(4):
        for jt in range(4):
            low = jy * 48 + jt * 12
            base = (t ^ jt) * 96 + (y ^ jy) * 24 + c * 12 - low
            source = jnp.where((row >= low) & (row < low + 12), row + base, source)
    pick = jnp.where(source == col, 1.0, 0.0).astype(BF)
    first = jnp.dot(pick, att_ref[...], preferred_element_type=F32).astype(BF)
    second = jnp.dot(pick, att2_ref[...], preferred_element_type=F32).astype(BF)
    both = jnp.concatenate([first, second], axis=1)
    for p in range(8):
        start = pl.multiple_of((rank_ref[3] ^ ORDER[p]) * COLS, 128)
        rows = slice(p * ROWS, (p + 1) * ROWS)
        rhs = jnp.concatenate([d_ref[rows, :], d2_ref[rows, :]], axis=0)
        part = jnp.dot(both, rhs, preferred_element_type=F32)
        own_ref[:, pl.ds(start, COLS)] = part[0:48]
        for j in range(3):
            out_refs[j][:, pl.ds(start, COLS)] = part[48 * (j + 1) : 48 * (j + 2)].astype(BF)


def backward_kernel(*refs):
    rank_ref, q_refs, kv_refs = refs[0], refs[1:5], refs[5:13]
    g_refs, stat_refs = refs[13:17], refs[17:21]
    dq_own, dq_other, own_ref, other_ref, bias_ref = refs[21:26]
    bias_ref[...] = log_counts(rank_ref, q_refs)
    for h in range(HEADS):
        cols = slice(h * HD, (h + 1) * HD)
        q = jnp.concatenate([r[0:ROWS, cols] for r in q_refs], axis=0)
        g = jnp.concatenate([r[cols, :] for r in g_refs], axis=1)
        log_total = jnp.concatenate([r[h : h + 1, :] for r in stat_refs], axis=1)
        delta = jnp.concatenate([r[3 + h : 4 + h, :] for r in stat_refs], axis=1)
        dq = jnp.zeros((HD, 4 * ROWS), F32)
        for b, kv in enumerate(kv_refs):
            k, v = kv[0:ROWS, cols], kv[ROWS : 2 * ROWS, cols]
            s = dot(k, q, 1, 1) * SCALE
            bias = [
                jnp.broadcast_to(bias_ref[2 * b + half : 2 * b + half + 1, :], (TILE, 4 * ROWS)) for half in range(2)
            ]
            p = jnp.exp(s + jnp.concatenate(bias, axis=0) - log_total)
            ds = (p * (jnp.dot(v, g, preferred_element_type=F32) - delta)).astype(BF)
            dv = dot(p.astype(BF), g, 1, 1)
            dk = jnp.dot(ds, q, preferred_element_type=F32) * SCALE
            dq = dq + dot(k, ds, 0, 0)
            place = (b % 4) * 2 * ROWS
            target = own_ref if b < 4 else other_ref
            target[place : place + ROWS, cols] = dk.astype(target.dtype)
            target[place + ROWS : place + 2 * ROWS, cols] = dv.astype(target.dtype)
        dq = dq * SCALE
        for j in range(4):
            target = dq_own if j < 2 else dq_other
            start = (j % 2) * COLS + h * HD
            target[start : start + HD, :] = dq[:, j * ROWS : (j + 1) * ROWS].astype(target.dtype)


def on_device(queries, keys, values, w_out, d_out, far_ids, far_counts):
    slab = lax.axis_index("slab")
    head = lax.axis_index("head")
    t, y, c = slab // 8, slab // 2 % 4, slab % 2
    ranks = jnp.stack([t, y, c, head]).astype(jnp.int32)

    q_ext, kv = call(
        pack_kernel,
        [((ROWS + 16, COLS), BF), ((2 * ROWS, COLS), BF)],
        far_ids,
        far_counts,
        queries,
        keys,
        values,
        flops=0,
        moved=10**6,
    )
    kv_near = [kv] + [swap(kv, "slab", 2 * e) for e in (1, 2, 3)]
    q_all = gathered(q_ext, "slab", 8)
    kv_all = kv_near + [swap(block, "slab", 1) for block in kv_near]

    d_out, _ = lax.optimization_barrier((d_out, kv_near[1]))
    d_full = jnp.concatenate([d_out, swap(d_out, "head", 4)], axis=0)
    d_full = jnp.concatenate([d_full, swap(d_full, "head", 1)], axis=0)
    d_full = jnp.concatenate([d_full, swap(d_full, "head", 2)], axis=0)
    d_other = swap(d_full, "slab", 1)

    grad = call(grad_kernel, [((COLS, ROWS), BF)], ranks, w_out, d_full, flops=3 * 10**8, moved=3 * 10**6)[0]
    g_all = gathered(grad, "slab", 8)

    bias_scratch = pltpu.VMEM((16, 4 * ROWS), F32)
    parts = call(
        forward_kernel,
        [((COLS + 16, ROWS), BF)] * 4,
        ranks,
        *q_all,
        *kv_all,
        flops=3 * 10**9,
        moved=3 * 10**6,
        scratch=[pltpu.VMEM((8 * ROWS, 4 * ROWS), F32), bias_scratch],
    )
    parts = [parts[0]] + [swap(parts[j], "slab", 8 * j) for j in (1, 2, 3)]
    att, stats = call(
        merge_kernel, [((COLS, ROWS), BF), ((8, ROWS), F32)], *parts, grad, flops=10**8, moved=10**6
    )
    stat_all = [stats] + [swap(stats, "slab", 8 * j) for j in (1, 2, 3)]
    att_other = swap(att, "slab", 1)

    mix = call(
        mix_kernel,
        [((4 * ROWS, COLS), F32), ((4 * ROWS, COLS), BF)],
        ranks,
        att,
        w_out,
        flops=3 * 10**8,
        moved=4 * 10**6,
    )
    mixed = mix[0] + swap(mix[1], "head", 2).astype(F32)
    mixed = mixed[: 2 * ROWS] + swap(mixed[2 * ROWS :].astype(BF), "head", 1).astype(F32)
    mixed = mixed[:ROWS] + swap(mixed[ROWS:].astype(BF), "head", 4).astype(F32)

    weight = call(
        weight_kernel,
        [((48, WIDE), F32)] + [((48, WIDE), BF)] * 3,
        ranks,
        att,
        att_other,
        d_full,
        d_other,
        flops=6 * 10**8,
        moved=4 * 10**6,
    )
    weight = weight[0] + sum((swap(weight[j], "slab", 2 * j).astype(F32) for j in (1, 2, 3)), 0.0)
    weight = weight[:24] + swap(weight[24:].astype(BF), "slab", 16).astype(F32)
    weight_grad = weight[:12] + swap(weight[12:].astype(BF), "slab", 8).astype(F32)

    dq_own, dq_other, own, other = call(
        backward_kernel,
        [((2 * COLS, ROWS), F32), ((2 * COLS, ROWS), BF), ((8 * ROWS, COLS), F32), ((8 * ROWS, COLS), BF)],
        ranks,
        *q_all,
        *kv_all,
        *g_all,
        *stat_all,
        flops=6 * 10**9,
        moved=6 * 10**6,
        scratch=[bias_scratch],
    )
    dq = dq_own + swap(dq_other, "slab", 16).astype(F32)
    dq = dq[:COLS] + swap(dq[COLS:].astype(BF), "slab", 8).astype(F32)
    query_grad = dq.astype(BF).T
    pair = (own + swap(other, "slab", 1).astype(F32)).reshape(4, 2 * ROWS, COLS)
    total = pair[0] + sum((swap(pair[e].astype(BF), "slab", 2 * e).astype(F32) for e in (1, 2, 3)), 0.0)
    total = total.astype(BF)
    return mixed.astype(BF), query_grad, total[:ROWS], total[ROWS:], weight_grad


def solution(mesh):
    placed = (
        P("slab", "head"),
        P("slab", "head"),
        P("slab", "head"),
        P("head", None),
        P("slab", "head"),
        P("slab", None),
        P("slab"),
    )
    return jax.shard_map(
        on_device,
        mesh=mesh,
        in_specs=placed,
        out_specs=(
            P("slab", "head"),
            P("slab", "head"),
            P("slab", "head"),
            P("slab", "head"),
            P(("head", "slab"), None),
        ),
        check_vma=False,
    )
```

```python
import functools
import math

import jax
import jax.numpy as jnp
from jax import lax
from jax.experimental import pallas as pl
from jax.experimental.pallas import tpu as pltpu
from jax.sharding import PartitionSpec as P

HD = 128
TILE = 64
HEADS = 3
ROWS = 128
COLS = 384
WIDE = 3072
NT_DEV = 4
NY_DEV = 4
DEAD = -1e30
SCALE = 1.0 / math.sqrt(HD)
ORDER = (0, 4, 1, 5, 2, 6, 3, 7)
BF = jnp.bfloat16
F32 = jnp.float32


def swap(block, axis, distance):
    devices = range(lax.axis_size(axis))
    return lax.ppermute(block, axis, [(i, i ^ distance) for i in devices])


def gathered(block, axis, unit):
    near = swap(block, axis, unit)
    rows = block.shape[0]
    far = swap(jnp.concatenate([block, near], axis=0), axis, 2 * unit)
    return [block, near, far[:rows], far[rows:]]


def dot(lhs, rhs, left, right):
    return lax.dot_general(lhs, rhs, (((left,), (right,)), ((), ())), preferred_element_type=F32)


def call(kernel, outs, *args, flops, moved, scratch=(), limit=24, by_hand=False):
    anywhere = pl.BlockSpec(memory_space=pl.ANY)
    vmem = pl.BlockSpec(memory_space=pltpu.VMEM)
    smem = pl.BlockSpec(memory_space=pltpu.SMEM)
    return pl.pallas_call(
        kernel,
        out_shape=[jax.ShapeDtypeStruct(shape, dtype) for shape, dtype in outs],
        in_specs=[anywhere if by_hand else smem if a.dtype == jnp.int32 else vmem for a in args],
        out_specs=[vmem] * len(outs),
        scratch_shapes=list(scratch),
        compiler_params=pltpu.CompilerParams(vmem_limit_bytes=limit * 1024 * 1024),
        cost_estimate=pl.CostEstimate(flops=1000, bytes_accessed=1000, transcendentals=0),
    )(*args)


def pack_kernel(ids_hbm, counts_hbm, q_hbm, k_hbm, v_hbm, q_out, kv_out, ids_ref, counts_ref, sems):
    copies = [
        pltpu.make_async_copy(ids_hbm, ids_ref, sems.at[0]),
        pltpu.make_async_copy(counts_hbm, counts_ref, sems.at[1]),
        pltpu.make_async_copy(k_hbm, kv_out.at[0:ROWS], sems.at[2]),
        pltpu.make_async_copy(v_hbm, kv_out.at[ROWS : 2 * ROWS], sems.at[3]),
        pltpu.make_async_copy(q_hbm, q_out.at[0:ROWS], sems.at[4]),
    ]
    for copy in copies:
        copy.start()
    copies[0].wait()
    copies[1].wait()
    row = lax.broadcasted_iota(jnp.int32, (16, COLS), 0)
    col = lax.broadcasted_iota(jnp.int32, (16, COLS), 1)
    named = jnp.full((16, COLS), -1.0, F32)
    for tile in range(2):
        for f in range(4):
            one = jnp.where(f < counts_ref[tile], ids_ref[tile, f], -1).astype(F32)
            named = jnp.where((row == tile) & (col == f), one, named)
    q_out[ROWS : ROWS + 16, :] = named.astype(BF)
    for copy in copies[2:]:
        copy.wait()


def after(value, *others):
    return lax.optimization_barrier((value, others))[0]


def log_counts(rank_ref, q_refs):
    t, y, c = rank_ref[0], rank_ref[1], rank_ref[2]
    row = lax.broadcasted_iota(jnp.int32, (16, ROWS), 0)
    lane = lax.broadcasted_iota(jnp.int32, (16, ROWS), 1)
    block = row // 2
    height = (y ^ (block % 4)) * 2 + (c ^ (block // 4))
    tile = (((t * 8 + height) * 2) + row % 2).astype(F32)
    near_height = jnp.abs(height - (y * 2 + c)) <= 1
    parts = []
    for j, q in enumerate(q_refs):
        near_time = jnp.abs((t ^ j) - t) <= 1
        count = jnp.where(near_height & near_time, 1.0, 0.0)
        named = q[ROWS : ROWS + 16, 0:HD].astype(F32)
        for f in range(4):
            one = jnp.where(lane < TILE, named[0:1, f : f + 1], named[1:2, f : f + 1])
            count = count + jnp.where(one == tile, 1.0, 0.0)
        parts.append(jnp.where(count > 0, jnp.log(jnp.maximum(count, 1.0)), DEAD))
    return jnp.concatenate(parts, axis=1)


def forward_kernel(*refs):
    rank_ref, q_refs, kv_refs = refs[0], refs[1:5], refs[5:13]
    out_refs, s_ref, bias_ref = refs[13:17], refs[17], refs[18]
    bias_ref[...] = log_counts(rank_ref, q_refs)
    row = lax.broadcasted_iota(jnp.int32, (16, 4 * ROWS), 0)
    stats = jnp.zeros((16, 4 * ROWS), F32)
    for h in range(HEADS):
        cols = slice(h * HD, (h + 1) * HD)
        q = jnp.concatenate([r[0:ROWS, cols] for r in q_refs], axis=0)
        top = jnp.full((1, 4 * ROWS), 2 * DEAD, F32)
        for b, kv in enumerate(kv_refs):
            s = dot(kv[0:ROWS, cols], q, 1, 1) * SCALE
            for half in range(2):
                part = s[half * TILE : (half + 1) * TILE] + bias_ref[2 * b + half : 2 * b + half + 1, :]
                start = b * ROWS + half * TILE
                s_ref[start : start + TILE, :] = part
                top = jnp.maximum(top, jnp.max(part, axis=0, keepdims=True))
        total = jnp.zeros((1, 4 * ROWS), F32)
        out = jnp.zeros((HD, 4 * ROWS), F32)
        for b, kv in enumerate(kv_refs):
            e = jnp.exp(s_ref[b * ROWS : (b + 1) * ROWS, :] - top)
            total = total + jnp.sum(e, axis=0, keepdims=True)
            out = out + dot(kv[ROWS : 2 * ROWS, cols], e.astype(BF), 0, 0)
        out = (out / total).astype(BF)
        for j, r in enumerate(out_refs):
            r[cols, :] = out[:, j * ROWS : (j + 1) * ROWS]
        rest = top + jnp.log(total)
        for piece in range(3):
            high = rest.astype(BF).astype(F32)
            stats = jnp.where(row == 3 * h + piece, high, stats)
            rest = rest - high
    stats = stats.astype(BF)
    for j, r in enumerate(out_refs):
        r[COLS : COLS + 16, :] = stats[:, j * ROWS : (j + 1) * ROWS]


def merge_kernel(*refs):
    parts, att_ref, logs_ref = refs[:4], refs[4], refs[5]
    row = lax.broadcasted_iota(jnp.int32, (8, ROWS), 0)
    merged = jnp.zeros((8, ROWS), F32)
    pieces = [r[COLS : COLS + 16, :].astype(F32) for r in parts]
    for h in range(HEADS):
        cols = slice(h * HD, (h + 1) * HD)
        logs = [(p[3 * h : 3 * h + 1] + p[3 * h + 1 : 3 * h + 2]) + p[3 * h + 2 : 3 * h + 3] for p in pieces]
        top = functools.reduce(jnp.maximum, logs)
        shares = [jnp.exp(l - top) for l in logs]
        total = functools.reduce(jnp.add, shares)
        out = sum((r[cols, :].astype(F32) * (w / total) for r, w in zip(parts, shares)), jnp.zeros((HD, ROWS), F32))
        att_ref[cols, :] = out.astype(BF)
        merged = jnp.where(row == h, top + jnp.log(total), merged)
    logs_ref[...] = merged


def delta_kernel(logs_ref, att_ref, grad_ref, stats_ref):
    row = lax.broadcasted_iota(jnp.int32, (8, ROWS), 0)
    stats = logs_ref[...]
    for h in range(HEADS):
        cols = slice(h * HD, (h + 1) * HD)
        delta = jnp.sum(att_ref[cols, :].astype(F32) * grad_ref[cols, :].astype(F32), axis=0, keepdims=True)
        stats = jnp.where(row == 3 + h, delta, stats)
    stats_ref[...] = stats


def grad_kernel(rank_ref, w_ref, d_ref, out_ref):
    total = jnp.zeros((COLS, ROWS), F32)
    for p in range(8):
        start = pl.multiple_of((rank_ref[3] ^ ORDER[p]) * COLS, 128)
        total = total + dot(w_ref[:, pl.ds(start, COLS)], d_ref[p * ROWS : (p + 1) * ROWS, :], 1, 1)
    out_ref[...] = total.astype(BF)


def mix_kernel(rank_ref, att_ref, w_ref, own_ref, other_ref):
    att = att_ref[...].T
    for i, p in enumerate(ORDER):
        start = pl.multiple_of((rank_ref[3] ^ p) * COLS, 128)
        part = jnp.dot(att, w_ref[:, pl.ds(start, COLS)], preferred_element_type=F32)
        target = own_ref if i < 4 else other_ref
        target[(i % 4) * ROWS : (i % 4 + 1) * ROWS, :] = part.astype(target.dtype)


def weight_kernel(rank_ref, att_ref, att2_ref, d_ref, d2_ref, own_ref, *out_refs):
    t, y, c = rank_ref[0], rank_ref[1], rank_ref[2]
    row = lax.broadcasted_iota(jnp.int32, (192, COLS), 0)
    col = lax.broadcasted_iota(jnp.int32, (192, COLS), 1)
    source = row * 0
    for jy in range(4):
        for jt in range(4):
            low = jy * 48 + jt * 12
            base = (t ^ jt) * 96 + (y ^ jy) * 24 + c * 12 - low
            source = jnp.where((row >= low) & (row < low + 12), row + base, source)
    pick = jnp.where(source == col, 1.0, 0.0).astype(BF)
    first = jnp.dot(pick, att_ref[...], preferred_element_type=F32).astype(BF)
    second = jnp.dot(pick, att2_ref[...], preferred_element_type=F32).astype(BF)
    both = jnp.concatenate([first, second], axis=1)
    for p in range(8):
        start = pl.multiple_of((rank_ref[3] ^ ORDER[p]) * COLS, 128)
        rows = slice(p * ROWS, (p + 1) * ROWS)
        rhs = jnp.concatenate([d_ref[rows, :], d2_ref[rows, :]], axis=0)
        part = jnp.dot(both, rhs, preferred_element_type=F32)
        own_ref[:, pl.ds(start, COLS)] = part[0:48]
        for j in range(3):
            out_refs[j][:, pl.ds(start, COLS)] = part[48 * (j + 1) : 48 * (j + 2)].astype(BF)


def backward_kernel(*refs):
    rank_ref, q_refs, kv_refs = refs[0], refs[1:5], refs[5:13]
    g_refs, stat_refs = refs[13:17], refs[17:21]
    dq_own, dq_other, own_ref, other_ref, bias_ref = refs[21:26]
    bias_ref[...] = log_counts(rank_ref, q_refs)
    for h in range(HEADS):
        cols = slice(h * HD, (h + 1) * HD)
        q = jnp.concatenate([r[0:ROWS, cols] for r in q_refs], axis=0)
        g = jnp.concatenate([r[cols, :] for r in g_refs], axis=1)
        log_total = jnp.concatenate([r[h : h + 1, :] for r in stat_refs], axis=1)
        delta = jnp.concatenate([r[3 + h : 4 + h, :] for r in stat_refs], axis=1)
        dq = jnp.zeros((HD, 4 * ROWS), F32)
        for b, kv in enumerate(kv_refs):
            k, v = kv[0:ROWS, cols], kv[ROWS : 2 * ROWS, cols]
            s = dot(k, q, 1, 1) * SCALE
            bias = [
                jnp.broadcast_to(bias_ref[2 * b + half : 2 * b + half + 1, :], (TILE, 4 * ROWS)) for half in range(2)
            ]
            p = jnp.exp(s + jnp.concatenate(bias, axis=0) - log_total)
            ds = (p * (jnp.dot(v, g, preferred_element_type=F32) - delta)).astype(BF)
            dv = dot(p.astype(BF), g, 1, 1)
            dk = jnp.dot(ds, q, preferred_element_type=F32) * SCALE
            dq = dq + dot(k, ds, 0, 0)
            place = (b % 4) * 2 * ROWS
            target = own_ref if b < 4 else other_ref
            target[place : place + ROWS, cols] = dk.astype(target.dtype)
            target[place + ROWS : place + 2 * ROWS, cols] = dv.astype(target.dtype)
        dq = dq * SCALE
        for j in range(4):
            target = dq_own if j < 2 else dq_other
            start = (j % 2) * COLS + h * HD
            target[start : start + HD, :] = dq[:, j * ROWS : (j + 1) * ROWS].astype(target.dtype)


def on_device(queries, keys, values, w_out, d_out, far_ids, far_counts):
    slab = lax.axis_index("slab")
    head = lax.axis_index("head")
    t, y, c = slab // 8, slab // 2 % 4, slab % 2
    ranks = jnp.stack([t, y, c, head]).astype(jnp.int32)

    d_across = swap(d_out, "head", 4)
    q_ext, kv = call(
        pack_kernel,
        [((ROWS + 16, COLS), BF), ((2 * ROWS, COLS), BF)],
        far_ids,
        far_counts,
        queries,
        keys,
        values,
        flops=0,
        moved=10**6,
        scratch=[pltpu.SMEM((2, 4), jnp.int32), pltpu.SMEM((2,), jnp.int32), pltpu.SemaphoreType.DMA((5,))],
        by_hand=True,
    )
    kv_near = [kv] + [swap(kv, "slab", 2 * e) for e in (1, 2, 3)]
    q_all = gathered(q_ext, "slab", 8)
    kv_all = kv_near + [swap(block, "slab", 1) for block in kv_near]

    d_full = after(jnp.concatenate([d_out, d_across], axis=0), *kv_near)
    d_full = jnp.concatenate([d_full, swap(d_full, "head", 1)], axis=0)
    d_full = jnp.concatenate([d_full, swap(d_full, "head", 2)], axis=0)

    bias_scratch = pltpu.VMEM((16, 4 * ROWS), F32)
    parts = call(
        forward_kernel,
        [((COLS + 16, ROWS), BF)] * 4,
        ranks,
        *q_all,
        *kv_all,
        flops=3 * 10**9,
        moved=3 * 10**6,
        scratch=[pltpu.VMEM((8 * ROWS, 4 * ROWS), F32), bias_scratch],
    )
    parts = [parts[0]] + [swap(parts[j], "slab", 8 * j) for j in (1, 2, 3)]
    d_full = after(d_full, parts[1])
    d_other = swap(d_full, "slab", 1)
    grad = call(grad_kernel, [((COLS, ROWS), BF)], ranks, w_out, d_full, flops=3 * 10**8, moved=3 * 10**6)[0]
    g_all = gathered(grad, "slab", 8)
    parts[0] = after(parts[0], g_all[1])
    att, logs = call(merge_kernel, [((COLS, ROWS), BF), ((8, ROWS), F32)], *parts, flops=10**8, moved=10**6)
    stats = call(delta_kernel, [((8, ROWS), F32)], logs, att, grad, flops=10**6, moved=10**6)[0]
    stat_all = [stats] + [swap(stats, "slab", 8 * j) for j in (1, 2, 3)]
    att_other = swap(att, "slab", 1)

    mix = call(
        mix_kernel,
        [((4 * ROWS, COLS), F32), ((4 * ROWS, COLS), BF)],
        ranks,
        att,
        w_out,
        flops=3 * 10**8,
        moved=4 * 10**6,
    )
    mix_in = swap(mix[1], "head", 2)
    weight = call(
        weight_kernel,
        [((48, WIDE), F32)] + [((48, WIDE), BF)] * 3,
        ranks,
        att,
        att_other,
        d_full,
        d_other,
        flops=6 * 10**8,
        moved=4 * 10**6,
    )
    weight_in = [swap(weight[j], "slab", 2 * j) for j in (1, 2, 3)]
    stat_all[0] = after(stat_all[0], weight[1])

    dq_own, dq_other, own, other = call(
        backward_kernel,
        [((2 * COLS, ROWS), F32), ((2 * COLS, ROWS), BF), ((8 * ROWS, COLS), F32), ((8 * ROWS, COLS), BF)],
        ranks,
        *q_all,
        *kv_all,
        *g_all,
        *stat_all,
        flops=6 * 10**9,
        moved=6 * 10**6,
        scratch=[bias_scratch],
    )
    weight = after(weight[0], other) + sum((w.astype(F32) for w in weight_in), 0.0)
    weight_away = weight[24:].astype(BF)
    mixed = after(mix[0], other) + mix_in.astype(F32)
    mixed_away = mixed[2 * ROWS :].astype(BF)

    other = swap(other, "slab", 1)
    pair = (after(own, weight_away, mixed_away) + other.astype(F32)).reshape(4, 2 * ROWS, COLS)
    away = [pair[e].astype(BF) for e in (1, 2, 3)]
    total = pair[0] + sum((swap(away[e - 1], "slab", 2 * e).astype(F32) for e in (1, 2, 3)), 0.0)
    total = total.astype(BF)

    weight = after(weight[:24], away[0]) + swap(weight_away, "slab", 16).astype(F32)
    weight_grad = weight[:12] + swap(weight[12:].astype(BF), "slab", 8).astype(F32)
    mixed = after(mixed[: 2 * ROWS], away[0]) + swap(mixed_away, "head", 1).astype(F32)
    mixed = mixed[:ROWS] + swap(mixed[ROWS:].astype(BF), "head", 4).astype(F32)

    dq = dq_own + swap(after(dq_other, away[0]), "slab", 16).astype(F32)
    dq = dq[:COLS] + swap(dq[COLS:].astype(BF), "slab", 8).astype(F32)
    query_grad = dq.astype(BF).T
    return mixed.astype(BF), query_grad, total[:ROWS], total[ROWS:], weight_grad


def solution(mesh):
    placed = (
        P("slab", "head"),
        P("slab", "head"),
        P("slab", "head"),
        P("head", None),
        P("slab", "head"),
        P("slab", None),
        P("slab"),
    )
    return jax.shard_map(
        on_device,
        mesh=mesh,
        in_specs=placed,
        out_specs=(
            P("slab", "head"),
            P("slab", "head"),
            P("slab", "head"),
            P("slab", "head"),
            P(("head", "slab"), None),
        ),
        check_vma=False,
    )
```

```python
import functools
import math

import jax
import jax.numpy as jnp
from jax import lax
from jax.experimental import pallas as pl
from jax.experimental.pallas import tpu as pltpu
from jax.sharding import PartitionSpec as P

HD = 128
TILE = 64
HEADS = 3
ROWS = 128
COLS = 384
WIDE = 3072
NT_DEV = 4
NY_DEV = 4
DEAD = -1e30
SCALE = 1.0 / math.sqrt(HD)
ORDER = (0, 4, 1, 5, 2, 6, 3, 7)
BF = jnp.bfloat16
F32 = jnp.float32


def swap(block, axis, distance):
    devices = range(lax.axis_size(axis))
    return lax.ppermute(block, axis, [(i, i ^ distance) for i in devices])


def gathered(block, axis, unit):
    near = swap(block, axis, unit)
    rows = block.shape[0]
    far = swap(jnp.concatenate([block, near], axis=0), axis, 2 * unit)
    return [block, near, far[:rows], far[rows:]]


def dot(lhs, rhs, left, right):
    return lax.dot_general(lhs, rhs, (((left,), (right,)), ((), ())), preferred_element_type=F32)


def call(kernel, outs, *args, flops, moved, scratch=(), limit=24, by_hand=False):
    anywhere = pl.BlockSpec(memory_space=pltpu.HBM)
    vmem = pl.BlockSpec(memory_space=pltpu.VMEM)
    smem = pl.BlockSpec(memory_space=pltpu.SMEM)
    return pl.pallas_call(
        kernel,
        out_shape=[jax.ShapeDtypeStruct(shape, dtype) for shape, dtype in outs],
        in_specs=[anywhere if by_hand else smem if a.dtype == jnp.int32 else vmem for a in args],
        out_specs=[vmem] * len(outs),
        scratch_shapes=list(scratch),
        compiler_params=pltpu.CompilerParams(vmem_limit_bytes=limit * 1024 * 1024),
        cost_estimate=pl.CostEstimate(flops=1000, bytes_accessed=1000, transcendentals=0),
    )(*args)


def pack_kernel(ids_hbm, counts_hbm, q_hbm, k_hbm, v_hbm, q_out, kv_out, ids_ref, counts_ref, sems):
    copies = [
        pltpu.make_async_copy(ids_hbm, ids_ref, sems.at[0]),
        pltpu.make_async_copy(counts_hbm, counts_ref, sems.at[1]),
        pltpu.make_async_copy(k_hbm, kv_out.at[0:ROWS], sems.at[2]),
        pltpu.make_async_copy(v_hbm, kv_out.at[ROWS : 2 * ROWS], sems.at[3]),
        pltpu.make_async_copy(q_hbm, q_out.at[0:ROWS], sems.at[4]),
    ]
    for copy in copies:
        copy.start()
    copies[0].wait()
    copies[1].wait()
    row = lax.broadcasted_iota(jnp.int32, (16, COLS), 0)
    col = lax.broadcasted_iota(jnp.int32, (16, COLS), 1)
    named = jnp.full((16, COLS), -1.0, F32)
    for tile in range(2):
        for f in range(4):
            one = jnp.where(f < counts_ref[tile], ids_ref[tile, f], -1).astype(F32)
            named = jnp.where((row == tile) & (col == f), one, named)
    q_out[ROWS : ROWS + 16, :] = named.astype(BF)
    for copy in copies[2:]:
        copy.wait()


def after(value, *others):
    return lax.optimization_barrier((value, others))[0]


def log_counts(rank_ref, q_refs):
    t, y, c = rank_ref[0], rank_ref[1], rank_ref[2]
    row = lax.broadcasted_iota(jnp.int32, (16, ROWS), 0)
    lane = lax.broadcasted_iota(jnp.int32, (16, ROWS), 1)
    block = row // 2
    height = (y ^ (block % 4)) * 2 + (c ^ (block // 4))
    tile = (((t * 8 + height) * 2) + row % 2).astype(F32)
    near_height = jnp.abs(height - (y * 2 + c)) <= 1
    parts = []
    for j, q in enumerate(q_refs):
        near_time = jnp.abs((t ^ j) - t) <= 1
        count = jnp.where(near_height & near_time, 1.0, 0.0)
        named = q[ROWS : ROWS + 16, 0:HD].astype(F32)
        for f in range(4):
            one = jnp.where(lane < TILE, named[0:1, f : f + 1], named[1:2, f : f + 1])
            count = count + jnp.where(one == tile, 1.0, 0.0)
        parts.append(jnp.where(count > 0, jnp.log(jnp.maximum(count, 1.0)), DEAD))
    return jnp.concatenate(parts, axis=1)


def forward_kernel(*refs):
    rank_ref, q_refs, kv_refs = refs[0], refs[1:5], refs[5:13]
    out_refs, s_ref, bias_ref = refs[13:17], refs[17], refs[18]
    bias_ref[...] = log_counts(rank_ref, q_refs)
    row = lax.broadcasted_iota(jnp.int32, (16, 4 * ROWS), 0)
    stats = jnp.zeros((16, 4 * ROWS), F32)
    for h in range(HEADS):
        cols = slice(h * HD, (h + 1) * HD)
        q = jnp.concatenate([r[0:ROWS, cols] for r in q_refs], axis=0)
        top = jnp.full((1, 4 * ROWS), 2 * DEAD, F32)
        for b, kv in enumerate(kv_refs):
            s = dot(kv[0:ROWS, cols], q, 1, 1) * SCALE
            for half in range(2):
                part = s[half * TILE : (half + 1) * TILE] + bias_ref[2 * b + half : 2 * b + half + 1, :]
                start = b * ROWS + half * TILE
                s_ref[start : start + TILE, :] = part
                top = jnp.maximum(top, jnp.max(part, axis=0, keepdims=True))
        total = jnp.zeros((1, 4 * ROWS), F32)
        out = jnp.zeros((HD, 4 * ROWS), F32)
        for b, kv in enumerate(kv_refs):
            e = jnp.exp(s_ref[b * ROWS : (b + 1) * ROWS, :] - top)
            total = total + jnp.sum(e, axis=0, keepdims=True)
            out = out + dot(kv[ROWS : 2 * ROWS, cols], e.astype(BF), 0, 0)
        out = (out / total).astype(BF)
        for j, r in enumerate(out_refs):
            r[cols, :] = out[:, j * ROWS : (j + 1) * ROWS]
        rest = top + jnp.log(total)
        for piece in range(3):
            high = rest.astype(BF).astype(F32)
            stats = jnp.where(row == 3 * h + piece, high, stats)
            rest = rest - high
    stats = stats.astype(BF)
    for j, r in enumerate(out_refs):
        r[COLS : COLS + 16, :] = stats[:, j * ROWS : (j + 1) * ROWS]


def merge_kernel(*refs):
    parts, att_ref, logs_ref = refs[:4], refs[4], refs[5]
    row = lax.broadcasted_iota(jnp.int32, (8, ROWS), 0)
    merged = jnp.zeros((8, ROWS), F32)
    pieces = [r[COLS : COLS + 16, :].astype(F32) for r in parts]
    for h in range(HEADS):
        cols = slice(h * HD, (h + 1) * HD)
        logs = [(p[3 * h : 3 * h + 1] + p[3 * h + 1 : 3 * h + 2]) + p[3 * h + 2 : 3 * h + 3] for p in pieces]
        top = functools.reduce(jnp.maximum, logs)
        shares = [jnp.exp(l - top) for l in logs]
        total = functools.reduce(jnp.add, shares)
        out = sum((r[cols, :].astype(F32) * (w / total) for r, w in zip(parts, shares)), jnp.zeros((HD, ROWS), F32))
        att_ref[cols, :] = out.astype(BF)
        merged = jnp.where(row == h, top + jnp.log(total), merged)
    logs_ref[...] = merged


def delta_kernel(logs_ref, att_ref, grad_ref, stats_ref):
    row = lax.broadcasted_iota(jnp.int32, (8, ROWS), 0)
    stats = logs_ref[...]
    for h in range(HEADS):
        cols = slice(h * HD, (h + 1) * HD)
        delta = jnp.sum(att_ref[cols, :].astype(F32) * grad_ref[cols, :].astype(F32), axis=0, keepdims=True)
        stats = jnp.where(row == 3 + h, delta, stats)
    stats_ref[...] = stats


def grad_kernel(rank_ref, w_ref, d_ref, out_ref):
    total = jnp.zeros((COLS, ROWS), F32)
    for p in range(8):
        start = pl.multiple_of((rank_ref[3] ^ ORDER[p]) * COLS, 128)
        total = total + dot(w_ref[:, pl.ds(start, COLS)], d_ref[p * ROWS : (p + 1) * ROWS, :], 1, 1)
    out_ref[...] = total.astype(BF)


def mix_kernel(rank_ref, att_ref, w_ref, own_ref, other_ref):
    att = att_ref[...].T
    for i, p in enumerate(ORDER):
        start = pl.multiple_of((rank_ref[3] ^ p) * COLS, 128)
        part = jnp.dot(att, w_ref[:, pl.ds(start, COLS)], preferred_element_type=F32)
        target = own_ref if i < 4 else other_ref
        target[(i % 4) * ROWS : (i % 4 + 1) * ROWS, :] = part.astype(target.dtype)


def weight_kernel(rank_ref, att_ref, att2_ref, d_ref, d2_ref, own_ref, *out_refs):
    t, y, c = rank_ref[0], rank_ref[1], rank_ref[2]
    row = lax.broadcasted_iota(jnp.int32, (192, COLS), 0)
    col = lax.broadcasted_iota(jnp.int32, (192, COLS), 1)
    source = row * 0
    for jy in range(4):
        for jt in range(4):
            low = jy * 48 + jt * 12
            base = (t ^ jt) * 96 + (y ^ jy) * 24 + c * 12 - low
            source = jnp.where((row >= low) & (row < low + 12), row + base, source)
    pick = jnp.where(source == col, 1.0, 0.0).astype(BF)
    first = jnp.dot(pick, att_ref[...], preferred_element_type=F32).astype(BF)
    second = jnp.dot(pick, att2_ref[...], preferred_element_type=F32).astype(BF)
    both = jnp.concatenate([first, second], axis=1)
    for p in range(8):
        start = pl.multiple_of((rank_ref[3] ^ ORDER[p]) * COLS, 128)
        rows = slice(p * ROWS, (p + 1) * ROWS)
        rhs = jnp.concatenate([d_ref[rows, :], d2_ref[rows, :]], axis=0)
        part = jnp.dot(both, rhs, preferred_element_type=F32)
        own_ref[:, pl.ds(start, COLS)] = part[0:48]
        for j in range(3):
            out_refs[j][:, pl.ds(start, COLS)] = part[48 * (j + 1) : 48 * (j + 2)].astype(BF)


def backward_kernel(*refs):
    rank_ref, q_refs, kv_refs = refs[0], refs[1:5], refs[5:13]
    g_refs, stat_refs = refs[13:17], refs[17:21]
    dq_own, dq_other, own_ref, other_ref, bias_ref = refs[21:26]
    bias_ref[...] = log_counts(rank_ref, q_refs)
    for h in range(HEADS):
        cols = slice(h * HD, (h + 1) * HD)
        q = jnp.concatenate([r[0:ROWS, cols] for r in q_refs], axis=0)
        g = jnp.concatenate([r[cols, :] for r in g_refs], axis=1)
        log_total = jnp.concatenate([r[h : h + 1, :] for r in stat_refs], axis=1)
        delta = jnp.concatenate([r[3 + h : 4 + h, :] for r in stat_refs], axis=1)
        dq = jnp.zeros((HD, 4 * ROWS), F32)
        for b, kv in enumerate(kv_refs):
            k, v = kv[0:ROWS, cols], kv[ROWS : 2 * ROWS, cols]
            s = dot(k, q, 1, 1) * SCALE
            bias = [
                jnp.broadcast_to(bias_ref[2 * b + half : 2 * b + half + 1, :], (TILE, 4 * ROWS)) for half in range(2)
            ]
            p = jnp.exp(s + jnp.concatenate(bias, axis=0) - log_total)
            ds = (p * (jnp.dot(v, g, preferred_element_type=F32) - delta)).astype(BF)
            dv = dot(p.astype(BF), g, 1, 1)
            dk = jnp.dot(ds, q, preferred_element_type=F32) * SCALE
            dq = dq + dot(k, ds, 0, 0)
            place = (b % 4) * 2 * ROWS
            target = own_ref if b < 4 else other_ref
            target[place : place + ROWS, cols] = dk.astype(target.dtype)
            target[place + ROWS : place + 2 * ROWS, cols] = dv.astype(target.dtype)
        dq = dq * SCALE
        for j in range(4):
            target = dq_own if j < 2 else dq_other
            start = (j % 2) * COLS + h * HD
            target[start : start + HD, :] = dq[:, j * ROWS : (j + 1) * ROWS].astype(target.dtype)


def on_device(queries, keys, values, w_out, d_out, far_ids, far_counts):
    slab = lax.axis_index("slab")
    head = lax.axis_index("head")
    t, y, c = slab // 8, slab // 2 % 4, slab % 2
    ranks = jnp.stack([t, y, c, head]).astype(jnp.int32)

    q_ext, kv = call(
        pack_kernel,
        [((ROWS + 16, COLS), BF), ((2 * ROWS, COLS), BF)],
        far_ids,
        far_counts,
        queries,
        keys,
        values,
        flops=0,
        moved=10**6,
        scratch=[pltpu.SMEM((2, 4), jnp.int32), pltpu.SMEM((2,), jnp.int32), pltpu.SemaphoreType.DMA((5,))],
        by_hand=True,
        limit=58,
    )
    kv_near = [kv] + [swap(kv, "slab", 2 * e) for e in (1, 2, 3)]
    q_all = gathered(q_ext, "slab", 8)
    kv_all = kv_near + [swap(block, "slab", 1) for block in kv_near]

    d_across = after(swap(after(d_out, q_all[1]), "head", 4), *kv_near)
    d_full = jnp.concatenate([d_out, d_across], axis=0)
    d_full = jnp.concatenate([d_full, swap(d_full, "head", 1)], axis=0)
    d_full = jnp.concatenate([d_full, swap(d_full, "head", 2)], axis=0)

    bias_scratch = pltpu.VMEM((16, 4 * ROWS), F32)
    parts = call(
        forward_kernel,
        [((COLS + 16, ROWS), BF)] * 4,
        ranks,
        *q_all,
        *kv_all,
        flops=3 * 10**9,
        moved=3 * 10**6,
        scratch=[pltpu.VMEM((8 * ROWS, 4 * ROWS), F32), bias_scratch],
    )
    parts = [parts[0]] + [swap(parts[j], "slab", 8 * j) for j in (1, 2, 3)]
    d_full = after(d_full, *parts[1:])
    d_other = swap(d_full, "slab", 1)
    grad = call(grad_kernel, [((COLS, ROWS), BF)], ranks, w_out, d_full, flops=3 * 10**8, moved=3 * 10**6)[0]
    g_all = gathered(grad, "slab", 8)
    parts[0] = after(parts[0], g_all[1])
    att, logs = call(merge_kernel, [((COLS, ROWS), BF), ((8, ROWS), F32)], *parts, flops=10**8, moved=10**6)
    stats = call(delta_kernel, [((8, ROWS), F32)], logs, att, grad, flops=10**6, moved=10**6)[0]
    stat_all = [stats] + [swap(stats, "slab", 8 * j) for j in (1, 2, 3)]
    att_other = swap(att, "slab", 1)

    mix = call(
        mix_kernel,
        [((4 * ROWS, COLS), F32), ((4 * ROWS, COLS), BF)],
        ranks,
        att,
        w_out,
        flops=3 * 10**8,
        moved=4 * 10**6,
    )
    mix_in = swap(mix[1], "head", 2)
    weight = call(
        weight_kernel,
        [((48, WIDE), F32)] + [((48, WIDE), BF)] * 3,
        ranks,
        att,
        att_other,
        d_full,
        d_other,
        flops=6 * 10**8,
        moved=4 * 10**6,
    )
    weight_in = [swap(weight[j], "slab", 2 * j) for j in (1, 2, 3)]
    stat_all[0] = after(stat_all[0], weight[1])

    dq_own, dq_other, own, other = call(
        backward_kernel,
        [((2 * COLS, ROWS), F32), ((2 * COLS, ROWS), BF), ((8 * ROWS, COLS), F32), ((8 * ROWS, COLS), BF)],
        ranks,
        *q_all,
        *kv_all,
        *g_all,
        *stat_all,
        flops=6 * 10**9,
        moved=6 * 10**6,
        scratch=[bias_scratch],
    )
    weight = after(weight[0], other) + sum((w.astype(F32) for w in weight_in), 0.0)
    weight_away = weight[24:].astype(BF)
    mixed = after(mix[0], other) + mix_in.astype(F32)
    mixed_away = mixed[2 * ROWS :].astype(BF)

    other = swap(other, "slab", 1)
    pair = (after(own, weight_away, mixed_away) + other.astype(F32)).reshape(4, 2 * ROWS, COLS)
    away = [pair[e].astype(BF) for e in (1, 2, 3)]
    arrived = [swap(away[e - 1], "slab", 2 * e) for e in (1, 2, 3)]
    dq_in = swap(after(dq_other, other), "slab", 16)

    weight = after(weight[:24], arrived[1]) + swap(weight_away, "slab", 16).astype(F32)
    weight_away = weight[12:].astype(BF)
    mixed = after(mixed[: 2 * ROWS], arrived[1]) + swap(mixed_away, "head", 1).astype(F32)
    mixed_away = mixed[ROWS:].astype(BF)
    dq = after(dq_own, arrived[1]) + dq_in.astype(F32)
    dq_away = dq[COLS:].astype(BF)

    total = after(pair[0], weight_away, mixed_away, dq_away) + sum((a.astype(F32) for a in arrived), 0.0)
    total = total.astype(BF)
    weight_grad = weight[:12] + swap(weight_away, "slab", 8).astype(F32)
    mixed = mixed[:ROWS] + swap(mixed_away, "head", 4).astype(F32)
    dq = dq[:COLS] + swap(dq_away, "slab", 8).astype(F32)
    query_grad = dq.astype(BF).T
    return mixed.astype(BF), query_grad, total[:ROWS], total[ROWS:], weight_grad


def solution(mesh):
    placed = (
        P("slab", "head"),
        P("slab", "head"),
        P("slab", "head"),
        P("head", None),
        P("slab", "head"),
        P("slab", None),
        P("slab"),
    )
    return jax.shard_map(
        on_device,
        mesh=mesh,
        in_specs=placed,
        out_specs=(
            P("slab", "head"),
            P("slab", "head"),
            P("slab", "head"),
            P("slab", "head"),
            P(("head", "slab"), None),
        ),
        check_vma=False,
    )
```

```python
import functools
import math

import jax
import jax.numpy as jnp
from jax import lax
from jax.experimental import pallas as pl
from jax.experimental.pallas import tpu as pltpu
from jax.sharding import PartitionSpec as P

HD = 128
TILE = 64
HEADS = 3
ROWS = 128
COLS = 384
WIDE = 3072
NT_DEV = 4
NY_DEV = 4
DEAD = -1e30
SCALE = 1.0 / math.sqrt(HD)
ORDER = (0, 4, 1, 5, 2, 6, 3, 7)
BF = jnp.bfloat16
F32 = jnp.float32


def swap(block, axis, distance):
    devices = range(lax.axis_size(axis))
    return lax.ppermute(block, axis, [(i, i ^ distance) for i in devices])


def dot(lhs, rhs, left, right):
    return lax.dot_general(lhs, rhs, (((left,), (right,)), ((), ())), preferred_element_type=F32)


def call(kernel, outs, *args, flops, moved, scratch=(), limit=24, by_hand=False):
    anywhere = pl.BlockSpec(memory_space=pltpu.HBM)
    vmem = pl.BlockSpec(memory_space=pltpu.VMEM)
    smem = pl.BlockSpec(memory_space=pltpu.SMEM)
    return pl.pallas_call(
        kernel,
        out_shape=[jax.ShapeDtypeStruct(shape, dtype) for shape, dtype in outs],
        in_specs=[anywhere if by_hand else smem if a.dtype == jnp.int32 else vmem for a in args],
        out_specs=[vmem] * len(outs),
        scratch_shapes=list(scratch),
        compiler_params=pltpu.CompilerParams(vmem_limit_bytes=limit * 1024 * 1024),
        cost_estimate=pl.CostEstimate(flops=1000, bytes_accessed=1000, transcendentals=0),
    )(*args)


def pack_kernel(ids_hbm, counts_hbm, q_hbm, k_hbm, v_hbm, q_out, kv_out, ids_ref, counts_ref, sems):
    copies = [
        pltpu.make_async_copy(ids_hbm, ids_ref, sems.at[0]),
        pltpu.make_async_copy(counts_hbm, counts_ref, sems.at[1]),
        pltpu.make_async_copy(k_hbm, kv_out.at[0:ROWS], sems.at[2]),
        pltpu.make_async_copy(v_hbm, kv_out.at[ROWS : 2 * ROWS], sems.at[3]),
        pltpu.make_async_copy(q_hbm, q_out.at[0:ROWS], sems.at[4]),
    ]
    for copy in copies:
        copy.start()
    copies[0].wait()
    copies[1].wait()
    row = lax.broadcasted_iota(jnp.int32, (16, COLS), 0)
    col = lax.broadcasted_iota(jnp.int32, (16, COLS), 1)
    named = jnp.full((16, COLS), -1.0, F32)
    for tile in range(2):
        for f in range(4):
            one = jnp.where(f < counts_ref[tile], ids_ref[tile, f], -1).astype(F32)
            named = jnp.where((row == tile) & (col == f), one, named)
    q_out[ROWS : ROWS + 16, :] = named.astype(BF)
    for copy in copies[2:]:
        copy.wait()


def after(value, *others):
    return lax.optimization_barrier((value, others))[0]


def log_counts(rank_ref, q_refs):
    t, y, c = rank_ref[0], rank_ref[1], rank_ref[2]
    row = lax.broadcasted_iota(jnp.int32, (16, ROWS), 0)
    lane = lax.broadcasted_iota(jnp.int32, (16, ROWS), 1)
    block = row // 2
    height = (y ^ (block % 4)) * 2 + (c ^ (block // 4))
    tile = (((t * 8 + height) * 2) + row % 2).astype(F32)
    near_height = jnp.abs(height - (y * 2 + c)) <= 1
    parts = []
    for j, q in enumerate(q_refs):
        near_time = jnp.abs((t ^ j) - t) <= 1
        count = jnp.where(near_height & near_time, 1.0, 0.0)
        named = q[ROWS : ROWS + 16, 0:HD].astype(F32)
        for f in range(4):
            one = jnp.where(lane < TILE, named[0:1, f : f + 1], named[1:2, f : f + 1])
            count = count + jnp.where(one == tile, 1.0, 0.0)
        parts.append(jnp.where(count > 0, jnp.log(jnp.maximum(count, 1.0)), DEAD))
    return jnp.concatenate(parts, axis=1)


def forward_kernel(*refs):
    rank_ref, q_refs, kv_refs = refs[0], refs[1:5], refs[5:13]
    out_refs, s_ref, bias_ref = refs[13:17], refs[17], refs[18]
    bias_ref[...] = log_counts(rank_ref, q_refs)
    row = lax.broadcasted_iota(jnp.int32, (16, 4 * ROWS), 0)
    stats = jnp.zeros((16, 4 * ROWS), F32)
    for h in range(HEADS):
        cols = slice(h * HD, (h + 1) * HD)
        q = jnp.concatenate([r[0:ROWS, cols] for r in q_refs], axis=0)
        top = jnp.full((1, 4 * ROWS), 2 * DEAD, F32)
        for b, kv in enumerate(kv_refs):
            s = dot(kv[0:ROWS, cols], q, 1, 1) * SCALE
            for half in range(2):
                part = s[half * TILE : (half + 1) * TILE] + bias_ref[2 * b + half : 2 * b + half + 1, :]
                start = b * ROWS + half * TILE
                s_ref[start : start + TILE, :] = part
                top = jnp.maximum(top, jnp.max(part, axis=0, keepdims=True))
        total = jnp.zeros((1, 4 * ROWS), F32)
        out = jnp.zeros((HD, 4 * ROWS), F32)
        for b, kv in enumerate(kv_refs):
            e = jnp.exp(s_ref[b * ROWS : (b + 1) * ROWS, :] - top)
            total = total + jnp.sum(e, axis=0, keepdims=True)
            out = out + dot(kv[ROWS : 2 * ROWS, cols], e.astype(BF), 0, 0)
        out = (out / total).astype(BF)
        for j, r in enumerate(out_refs):
            r[cols, :] = out[:, j * ROWS : (j + 1) * ROWS]
        rest = top + jnp.log(total)
        for piece in range(3):
            high = rest.astype(BF).astype(F32)
            stats = jnp.where(row == 3 * h + piece, high, stats)
            rest = rest - high
    stats = stats.astype(BF)
    for j, r in enumerate(out_refs):
        r[COLS : COLS + 16, :] = stats[:, j * ROWS : (j + 1) * ROWS]


def merge_kernel(*refs):
    parts, att_ref, logs_ref = refs[:4], refs[4], refs[5]
    row = lax.broadcasted_iota(jnp.int32, (8, ROWS), 0)
    merged = jnp.zeros((8, ROWS), F32)
    pieces = [r[COLS : COLS + 16, :].astype(F32) for r in parts]
    for h in range(HEADS):
        cols = slice(h * HD, (h + 1) * HD)
        logs = [(p[3 * h : 3 * h + 1] + p[3 * h + 1 : 3 * h + 2]) + p[3 * h + 2 : 3 * h + 3] for p in pieces]
        top = functools.reduce(jnp.maximum, logs)
        shares = [jnp.exp(l - top) for l in logs]
        total = functools.reduce(jnp.add, shares)
        out = sum((r[cols, :].astype(F32) * (w / total) for r, w in zip(parts, shares)), jnp.zeros((HD, ROWS), F32))
        att_ref[cols, :] = out.astype(BF)
        merged = jnp.where(row == h, top + jnp.log(total), merged)
    logs_ref[...] = merged


def delta_kernel(logs_ref, att_ref, grad_ref, stats_ref):
    row = lax.broadcasted_iota(jnp.int32, (8, ROWS), 0)
    stats = logs_ref[...]
    for h in range(HEADS):
        cols = slice(h * HD, (h + 1) * HD)
        delta = jnp.sum(att_ref[cols, :].astype(F32) * grad_ref[cols, :].astype(F32), axis=0, keepdims=True)
        stats = jnp.where(row == 3 + h, delta, stats)
    stats_ref[...] = stats


def grad_kernel(rank_ref, w_ref, d_ref, out_ref):
    total = jnp.zeros((COLS, ROWS), F32)
    for p in range(8):
        start = pl.multiple_of((rank_ref[3] ^ ORDER[p]) * COLS, 128)
        total = total + dot(w_ref[:, pl.ds(start, COLS)], d_ref[p * ROWS : (p + 1) * ROWS, :], 1, 1)
    out_ref[...] = total.astype(BF)


def mix_kernel(rank_ref, att_ref, w_ref, own_ref, other_ref):
    att = att_ref[...].T
    for i, p in enumerate(ORDER):
        start = pl.multiple_of((rank_ref[3] ^ p) * COLS, 128)
        part = jnp.dot(att, w_ref[:, pl.ds(start, COLS)], preferred_element_type=F32)
        target = own_ref if i < 4 else other_ref
        target[(i % 4) * ROWS : (i % 4 + 1) * ROWS, :] = part.astype(target.dtype)


def weight_kernel(rank_ref, att_ref, att2_ref, d_ref, d2_ref, own_ref, *out_refs):
    t, y, c = rank_ref[0], rank_ref[1], rank_ref[2]
    row = lax.broadcasted_iota(jnp.int32, (192, COLS), 0)
    col = lax.broadcasted_iota(jnp.int32, (192, COLS), 1)
    source = row * 0
    for jy in range(4):
        for jt in range(4):
            low = jy * 48 + jt * 12
            base = (t ^ jt) * 96 + (y ^ jy) * 24 + c * 12 - low
            source = jnp.where((row >= low) & (row < low + 12), row + base, source)
    pick = jnp.where(source == col, 1.0, 0.0).astype(BF)
    first = jnp.dot(pick, att_ref[...], preferred_element_type=F32).astype(BF)
    second = jnp.dot(pick, att2_ref[...], preferred_element_type=F32).astype(BF)
    both = jnp.concatenate([first, second], axis=1)
    for p in range(8):
        start = pl.multiple_of((rank_ref[3] ^ ORDER[p]) * COLS, 128)
        rows = slice(p * ROWS, (p + 1) * ROWS)
        rhs = jnp.concatenate([d_ref[rows, :], d2_ref[rows, :]], axis=0)
        part = jnp.dot(both, rhs, preferred_element_type=F32)
        own_ref[:, pl.ds(start, COLS)] = part[0:48]
        for j in range(3):
            out_refs[j][:, pl.ds(start, COLS)] = part[48 * (j + 1) : 48 * (j + 2)].astype(BF)


def backward_kernel(*refs):
    rank_ref, q_refs, kv_refs = refs[0], refs[1:5], refs[5:13]
    g_refs, stat_refs = refs[13:17], refs[17:21]
    dq_own, dq_other, own_ref, other_ref, bias_ref = refs[21:26]
    bias_ref[...] = log_counts(rank_ref, q_refs)
    for h in range(HEADS):
        cols = slice(h * HD, (h + 1) * HD)
        q = jnp.concatenate([r[0:ROWS, cols] for r in q_refs], axis=0)
        g = jnp.concatenate([r[cols, :] for r in g_refs], axis=1)
        log_total = jnp.concatenate([r[h : h + 1, :] for r in stat_refs], axis=1)
        delta = jnp.concatenate([r[3 + h : 4 + h, :] for r in stat_refs], axis=1)
        dq = jnp.zeros((HD, 4 * ROWS), F32)
        for b, kv in enumerate(kv_refs):
            k, v = kv[0:ROWS, cols], kv[ROWS : 2 * ROWS, cols]
            s = dot(k, q, 1, 1) * SCALE
            bias = [
                jnp.broadcast_to(bias_ref[2 * b + half : 2 * b + half + 1, :], (TILE, 4 * ROWS)) for half in range(2)
            ]
            p = jnp.exp(s + jnp.concatenate(bias, axis=0) - log_total)
            ds = (p * (jnp.dot(v, g, preferred_element_type=F32) - delta)).astype(BF)
            dv = dot(p.astype(BF), g, 1, 1)
            dk = jnp.dot(ds, q, preferred_element_type=F32) * SCALE
            dq = dq + dot(k, ds, 0, 0)
            place = (b % 4) * 2 * ROWS
            target = own_ref if b < 4 else other_ref
            target[place : place + ROWS, cols] = dk.astype(target.dtype)
            target[place + ROWS : place + 2 * ROWS, cols] = dv.astype(target.dtype)
        dq = dq * SCALE
        for j in range(4):
            target = dq_own if j < 2 else dq_other
            start = (j % 2) * COLS + h * HD
            target[start : start + HD, :] = dq[:, j * ROWS : (j + 1) * ROWS].astype(target.dtype)


def on_device(queries, keys, values, w_out, d_out, far_ids, far_counts):
    slab = lax.axis_index("slab")
    head = lax.axis_index("head")
    t, y, c = slab // 8, slab // 2 % 4, slab % 2
    ranks = jnp.stack([t, y, c, head]).astype(jnp.int32)

    q_ext, kv = call(
        pack_kernel,
        [((ROWS + 16, COLS), BF), ((2 * ROWS, COLS), BF)],
        far_ids,
        far_counts,
        queries,
        keys,
        values,
        flops=0,
        moved=10**6,
        scratch=[pltpu.SMEM((2, 4), jnp.int32), pltpu.SMEM((2,), jnp.int32), pltpu.SemaphoreType.DMA((5,))],
        by_hand=True,
        limit=58,
    )
    kv_near = [kv] + [swap(kv, "slab", 2 * e) for e in (1, 2, 3)]
    q_all = [q_ext] + [swap(q_ext, "slab", 8 * j) for j in (1, 2, 3)]
    kv_all = kv_near + [swap(block, "slab", 1) for block in kv_near]

    d_across = after(swap(after(d_out, q_all[1]), "head", 4), *kv_near, *q_all)
    d_full = jnp.concatenate([d_out, d_across], axis=0)
    d_near = swap(d_full, "head", 1)

    bias_scratch = pltpu.VMEM((16, 4 * ROWS), F32)
    parts = call(
        forward_kernel,
        [((COLS + 16, ROWS), BF)] * 4,
        ranks,
        *q_all,
        *kv_all,
        flops=3 * 10**9,
        moved=3 * 10**6,
        scratch=[pltpu.VMEM((8 * ROWS, 4 * ROWS), F32), bias_scratch],
    )
    d_full = jnp.concatenate([d_full, after(d_near, parts[0])], axis=0)
    d_full = jnp.concatenate([d_full, swap(d_full, "head", 2)], axis=0)
    parts = [parts[0]] + [swap(parts[j], "slab", 8 * j) for j in (1, 2, 3)]
    d_full = after(d_full, *parts[1:])
    d_other = swap(d_full, "slab", 1)
    grad = call(grad_kernel, [((COLS, ROWS), BF)], ranks, w_out, d_full, flops=3 * 10**8, moved=3 * 10**6)[0]
    g_near = swap(grad, "slab", 8)
    att, logs = call(merge_kernel, [((COLS, ROWS), BF), ((8, ROWS), F32)], *parts, flops=10**8, moved=10**6)
    stats = call(delta_kernel, [((8, ROWS), F32)], logs, att, grad, flops=10**6, moved=10**6)[0]
    stat_all = [stats] + [swap(stats, "slab", 8 * j) for j in (1, 2, 3)]
    att_other = swap(att, "slab", 1)

    mix = call(
        mix_kernel,
        [((4 * ROWS, COLS), F32), ((4 * ROWS, COLS), BF)],
        ranks,
        after(att, grad),
        w_out,
        flops=3 * 10**8,
        moved=4 * 10**6,
    )
    mix_in = swap(mix[1], "head", 2)
    g_far = swap(jnp.concatenate([grad, after(g_near, mix[1])], axis=0), "slab", 16)
    g_all = [grad, g_near, g_far[:COLS], g_far[COLS:]]
    weight = call(
        weight_kernel,
        [((48, WIDE), F32)] + [((48, WIDE), BF)] * 3,
        ranks,
        att,
        att_other,
        d_full,
        d_other,
        flops=6 * 10**8,
        moved=4 * 10**6,
    )
    weight_in = [swap(weight[j], "slab", 2 * j) for j in (1, 2, 3)]
    mixed = mix[0] + mix_in.astype(F32)
    mixed_away = mixed[2 * ROWS :].astype(BF)
    stat_all[0] = after(stat_all[0], weight[1], mixed_away)

    dq_own, dq_other, own, other = call(
        backward_kernel,
        [((2 * COLS, ROWS), F32), ((2 * COLS, ROWS), BF), ((8 * ROWS, COLS), F32), ((8 * ROWS, COLS), BF)],
        ranks,
        *q_all,
        *kv_all,
        *g_all,
        *stat_all,
        flops=6 * 10**9,
        moved=6 * 10**6,
        scratch=[bias_scratch],
    )
    weight = after(weight[0], other) + sum((w.astype(F32) for w in weight_in), 0.0)
    weight_away = weight[24:].astype(BF)

    other = swap(other, "slab", 1)
    pair = (after(own, weight_away) + other.astype(F32)).reshape(4, 2 * ROWS, COLS)
    away = [pair[e].astype(BF) for e in (1, 2, 3)]
    arrived = [swap(away[e - 1], "slab", 2 * e) for e in (1, 2, 3)]
    dq_in = swap(after(dq_other, other), "slab", 16)

    mixed = after(mixed[: 2 * ROWS], arrived[1]) + swap(mixed_away, "head", 1).astype(F32)
    mixed_away = mixed[ROWS:].astype(BF)
    weight = after(weight[:24], mixed_away) + swap(weight_away, "slab", 16).astype(F32)
    weight_away = weight[12:].astype(BF)
    dq = after(dq_own, mixed_away) + dq_in.astype(F32)
    dq_away = dq[COLS:].astype(BF)

    total = after(pair[0], weight_away, mixed_away, dq_away) + sum((a.astype(F32) for a in arrived), 0.0)
    total = total.astype(BF)
    weight_grad = weight[:12] + swap(weight_away, "slab", 8).astype(F32)
    mixed = mixed[:ROWS] + swap(mixed_away, "head", 4).astype(F32)
    dq = dq[:COLS] + swap(dq_away, "slab", 8).astype(F32)
    query_grad = dq.astype(BF).T
    return mixed.astype(BF), query_grad, total[:ROWS], total[ROWS:], weight_grad


def solution(mesh):
    placed = (
        P("slab", "head"),
        P("slab", "head"),
        P("slab", "head"),
        P("head", None),
        P("slab", "head"),
        P("slab", None),
        P("slab"),
    )
    return jax.shard_map(
        on_device,
        mesh=mesh,
        in_specs=placed,
        out_specs=(
            P("slab", "head"),
            P("slab", "head"),
            P("slab", "head"),
            P("slab", "head"),
            P(("head", "slab"), None),
        ),
        check_vma=False,
    )
```

```python
import functools
import math

import jax
import jax.numpy as jnp
from jax import lax
from jax.experimental import pallas as pl
from jax.experimental.pallas import tpu as pltpu
from jax.sharding import PartitionSpec as P

HD = 128
TILE = 64
HEADS = 3
ROWS = 128
COLS = 384
WIDE = 3072
NT_DEV = 4
NY_DEV = 4
DEAD = -1e30
SCALE = 1.0 / math.sqrt(HD)
ORDER = (0, 4, 1, 5, 2, 6, 3, 7)
BF = jnp.bfloat16
F32 = jnp.float32


def swap(block, axis, distance):
    devices = range(lax.axis_size(axis))
    return lax.ppermute(block, axis, [(i, i ^ distance) for i in devices])


def dot(lhs, rhs, left, right):
    return lax.dot_general(lhs, rhs, (((left,), (right,)), ((), ())), preferred_element_type=F32)


def call(kernel, outs, *args, flops, moved, scratch=(), limit=24, by_hand=False):
    anywhere = pl.BlockSpec(memory_space=pltpu.HBM)
    vmem = pl.BlockSpec(memory_space=pltpu.VMEM)
    smem = pl.BlockSpec(memory_space=pltpu.SMEM)
    return pl.pallas_call(
        kernel,
        out_shape=[jax.ShapeDtypeStruct(shape, dtype) for shape, dtype in outs],
        in_specs=[anywhere if by_hand else smem if a.dtype == jnp.int32 else vmem for a in args],
        out_specs=[vmem] * len(outs),
        scratch_shapes=list(scratch),
        compiler_params=pltpu.CompilerParams(vmem_limit_bytes=limit * 1024 * 1024),
        cost_estimate=pl.CostEstimate(flops=1000, bytes_accessed=1000, transcendentals=0),
    )(*args)


def pack_kernel(ids_hbm, counts_hbm, q_hbm, k_hbm, v_hbm, q_out, kv_out, ids_ref, counts_ref, sems):
    copies = [
        pltpu.make_async_copy(ids_hbm, ids_ref, sems.at[0]),
        pltpu.make_async_copy(counts_hbm, counts_ref, sems.at[1]),
        pltpu.make_async_copy(k_hbm, kv_out.at[0:ROWS], sems.at[2]),
        pltpu.make_async_copy(v_hbm, kv_out.at[ROWS : 2 * ROWS], sems.at[3]),
        pltpu.make_async_copy(q_hbm, q_out.at[0:ROWS], sems.at[4]),
    ]
    for copy in copies:
        copy.start()
    copies[0].wait()
    copies[1].wait()
    row = lax.broadcasted_iota(jnp.int32, (16, COLS), 0)
    col = lax.broadcasted_iota(jnp.int32, (16, COLS), 1)
    named = jnp.full((16, COLS), -1.0, F32)
    for tile in range(2):
        for f in range(4):
            one = jnp.where(f < counts_ref[tile], ids_ref[tile, f], -1).astype(F32)
            named = jnp.where((row == tile) & (col == f), one, named)
    q_out[ROWS : ROWS + 16, :] = named.astype(BF)
    for copy in copies[2:]:
        copy.wait()


def after(value, *others):
    return lax.optimization_barrier((value, others))[0]


def log_counts(rank_ref, q_refs):
    t, y, c = rank_ref[0], rank_ref[1], rank_ref[2]
    row = lax.broadcasted_iota(jnp.int32, (16, ROWS), 0)
    lane = lax.broadcasted_iota(jnp.int32, (16, ROWS), 1)
    block = row // 2
    height = (y ^ (block % 4)) * 2 + (c ^ (block // 4))
    tile = (((t * 8 + height) * 2) + row % 2).astype(F32)
    near_height = jnp.abs(height - (y * 2 + c)) <= 1
    parts = []
    for j, q in enumerate(q_refs):
        near_time = jnp.abs((t ^ j) - t) <= 1
        count = jnp.where(near_height & near_time, 1.0, 0.0)
        named = q[ROWS : ROWS + 16, 0:HD].astype(F32)
        for f in range(4):
            one = jnp.where(lane < TILE, named[0:1, f : f + 1], named[1:2, f : f + 1])
            count = count + jnp.where(one == tile, 1.0, 0.0)
        parts.append(jnp.where(count > 0, jnp.log(jnp.maximum(count, 1.0)), DEAD))
    return jnp.concatenate(parts, axis=1)


def forward_kernel(*refs):
    rank_ref, q_refs, kv_refs = refs[0], refs[1:5], refs[5:13]
    out_refs, s_ref, bias_ref = refs[13:17], refs[17], refs[18]
    bias_ref[...] = log_counts(rank_ref, q_refs)
    row = lax.broadcasted_iota(jnp.int32, (16, 4 * ROWS), 0)
    stats = jnp.zeros((16, 4 * ROWS), F32)
    for h in range(HEADS):
        cols = slice(h * HD, (h + 1) * HD)
        q = jnp.concatenate([r[0:ROWS, cols] for r in q_refs], axis=0)
        top = jnp.full((1, 4 * ROWS), 2 * DEAD, F32)
        for b, kv in enumerate(kv_refs):
            s = dot(kv[0:ROWS, cols], q, 1, 1) * SCALE
            for half in range(2):
                part = s[half * TILE : (half + 1) * TILE] + bias_ref[2 * b + half : 2 * b + half + 1, :]
                start = b * ROWS + half * TILE
                s_ref[start : start + TILE, :] = part
                top = jnp.maximum(top, jnp.max(part, axis=0, keepdims=True))
        total = jnp.zeros((1, 4 * ROWS), F32)
        out = jnp.zeros((HD, 4 * ROWS), F32)
        for b, kv in enumerate(kv_refs):
            e = jnp.exp(s_ref[b * ROWS : (b + 1) * ROWS, :] - top)
            total = total + jnp.sum(e, axis=0, keepdims=True)
            out = out + dot(kv[ROWS : 2 * ROWS, cols], e.astype(BF), 0, 0)
        out = (out / total).astype(BF)
        for j, r in enumerate(out_refs):
            r[cols, :] = out[:, j * ROWS : (j + 1) * ROWS]
        rest = top + jnp.log(total)
        for piece in range(3):
            high = rest.astype(BF).astype(F32)
            stats = jnp.where(row == 3 * h + piece, high, stats)
            rest = rest - high
    stats = stats.astype(BF)
    for j, r in enumerate(out_refs):
        r[COLS : COLS + 16, :] = stats[:, j * ROWS : (j + 1) * ROWS]


def merge_kernel(*refs):
    parts, att_ref, logs_ref = refs[:4], refs[4], refs[5]
    row = lax.broadcasted_iota(jnp.int32, (8, ROWS), 0)
    merged = jnp.zeros((8, ROWS), F32)
    pieces = [r[COLS : COLS + 16, :].astype(F32) for r in parts]
    for h in range(HEADS):
        cols = slice(h * HD, (h + 1) * HD)
        logs = [(p[3 * h : 3 * h + 1] + p[3 * h + 1 : 3 * h + 2]) + p[3 * h + 2 : 3 * h + 3] for p in pieces]
        top = functools.reduce(jnp.maximum, logs)
        shares = [jnp.exp(l - top) for l in logs]
        total = functools.reduce(jnp.add, shares)
        out = sum((r[cols, :].astype(F32) * (w / total) for r, w in zip(parts, shares)), jnp.zeros((HD, ROWS), F32))
        att_ref[cols, :] = out.astype(BF)
        merged = jnp.where(row == h, top + jnp.log(total), merged)
    logs_ref[...] = merged


def delta_kernel(logs_ref, att_ref, grad_ref, stats_ref):
    row = lax.broadcasted_iota(jnp.int32, (8, ROWS), 0)
    stats = logs_ref[...]
    for h in range(HEADS):
        cols = slice(h * HD, (h + 1) * HD)
        delta = jnp.sum(att_ref[cols, :].astype(F32) * grad_ref[cols, :].astype(F32), axis=0, keepdims=True)
        stats = jnp.where(row == 3 + h, delta, stats)
    stats_ref[...] = stats


def grad_kernel(rank_ref, w_ref, d_ref, out_ref):
    total = jnp.zeros((COLS, ROWS), F32)
    for p in range(8):
        start = pl.multiple_of((rank_ref[3] ^ ORDER[p]) * COLS, 128)
        total = total + dot(w_ref[:, pl.ds(start, COLS)], d_ref[p * ROWS : (p + 1) * ROWS, :], 1, 1)
    out_ref[...] = total.astype(BF)


def mix_kernel(rank_ref, att_ref, w_ref, own_ref, other_ref):
    att = att_ref[...].T
    for i, p in enumerate(ORDER):
        start = pl.multiple_of((rank_ref[3] ^ p) * COLS, 128)
        part = jnp.dot(att, w_ref[:, pl.ds(start, COLS)], preferred_element_type=F32)
        target = own_ref if i < 4 else other_ref
        target[(i % 4) * ROWS : (i % 4 + 1) * ROWS, :] = part.astype(target.dtype)


def weight_kernel(rank_ref, att_ref, att2_ref, d_ref, d2_ref, own_ref, *out_refs):
    t, y, c = rank_ref[0], rank_ref[1], rank_ref[2]
    row = lax.broadcasted_iota(jnp.int32, (192, COLS), 0)
    col = lax.broadcasted_iota(jnp.int32, (192, COLS), 1)
    source = row * 0
    for jy in range(4):
        for jt in range(4):
            low = jy * 48 + jt * 12
            base = (t ^ jt) * 96 + (y ^ jy) * 24 + c * 12 - low
            source = jnp.where((row >= low) & (row < low + 12), row + base, source)
    pick = jnp.where(source == col, 1.0, 0.0).astype(BF)
    first = jnp.dot(pick, att_ref[...], preferred_element_type=F32).astype(BF)
    second = jnp.dot(pick, att2_ref[...], preferred_element_type=F32).astype(BF)
    both = jnp.concatenate([first, second], axis=1)
    for p in range(8):
        start = pl.multiple_of((rank_ref[3] ^ ORDER[p]) * COLS, 128)
        rows = slice(p * ROWS, (p + 1) * ROWS)
        rhs = jnp.concatenate([d_ref[rows, :], d2_ref[rows, :]], axis=0)
        part = jnp.dot(both, rhs, preferred_element_type=F32)
        own_ref[:, pl.ds(start, COLS)] = part[0:48]
        for j in range(3):
            out_refs[j][:, pl.ds(start, COLS)] = part[48 * (j + 1) : 48 * (j + 2)].astype(BF)


def backward_kernel(*refs):
    rank_ref, q_refs, kv_refs = refs[0], refs[1:5], refs[5:13]
    g_refs, stat_refs = refs[13:17], refs[17:21]
    dq_own, dq_other, own_ref, other_ref, bias_ref = refs[21:26]
    bias_ref[...] = log_counts(rank_ref, q_refs)
    for h in range(HEADS):
        cols = slice(h * HD, (h + 1) * HD)
        q = jnp.concatenate([r[0:ROWS, cols] for r in q_refs], axis=0)
        g = jnp.concatenate([r[cols, :] for r in g_refs], axis=1)
        log_total = jnp.concatenate([r[h : h + 1, :] for r in stat_refs], axis=1)
        delta = jnp.concatenate([r[3 + h : 4 + h, :] for r in stat_refs], axis=1)
        dq = jnp.zeros((HD, 4 * ROWS), F32)
        for b, kv in enumerate(kv_refs):
            k, v = kv[0:ROWS, cols], kv[ROWS : 2 * ROWS, cols]
            s = dot(k, q, 1, 1) * SCALE
            bias = [
                jnp.broadcast_to(bias_ref[2 * b + half : 2 * b + half + 1, :], (TILE, 4 * ROWS)) for half in range(2)
            ]
            p = jnp.exp(s + jnp.concatenate(bias, axis=0) - log_total)
            ds = (p * (jnp.dot(v, g, preferred_element_type=F32) - delta)).astype(BF)
            dv = dot(p.astype(BF), g, 1, 1)
            dk = jnp.dot(ds, q, preferred_element_type=F32) * SCALE
            dq = dq + dot(k, ds, 0, 0)
            place = (b % 4) * 2 * ROWS
            target = own_ref if b < 4 else other_ref
            target[place : place + ROWS, cols] = dk.astype(target.dtype)
            target[place + ROWS : place + 2 * ROWS, cols] = dv.astype(target.dtype)
        dq = dq * SCALE
        for j in range(4):
            target = dq_own if j < 2 else dq_other
            start = (j % 2) * COLS + h * HD
            target[start : start + HD, :] = dq[:, j * ROWS : (j + 1) * ROWS].astype(target.dtype)


def on_device(queries, keys, values, w_out, d_out, far_ids, far_counts):
    slab = lax.axis_index("slab")
    head = lax.axis_index("head")
    t, y, c = slab // 8, slab // 2 % 4, slab % 2
    ranks = jnp.stack([t, y, c, head]).astype(jnp.int32)

    q_ext, kv = call(
        pack_kernel,
        [((ROWS + 16, COLS), BF), ((2 * ROWS, COLS), BF)],
        far_ids,
        far_counts,
        queries,
        keys,
        values,
        flops=0,
        moved=10**6,
        scratch=[pltpu.SMEM((2, 4), jnp.int32), pltpu.SMEM((2,), jnp.int32), pltpu.SemaphoreType.DMA((5,))],
        by_hand=True,
        limit=58,
    )
    kv_near = [kv] + [swap(kv, "slab", 2 * e) for e in (1, 2, 3)]
    q_all = [q_ext] + [swap(q_ext, "slab", 8 * j) for j in (1, 2, 3)]
    kv_all = kv_near + [swap(block, "slab", 1) for block in kv_near]

    d_across = after(swap(after(d_out, q_all[1]), "head", 4), *kv_near, *q_all)
    d_full = jnp.concatenate([d_out, d_across], axis=0)
    d_near = swap(d_full, "head", 1)

    bias_scratch = pltpu.VMEM((16, 4 * ROWS), F32)
    parts = call(
        forward_kernel,
        [((COLS + 16, ROWS), BF)] * 4,
        ranks,
        *q_all,
        *kv_all,
        flops=3 * 10**9,
        moved=3 * 10**6,
        scratch=[pltpu.VMEM((8 * ROWS, 4 * ROWS), F32), bias_scratch],
    )
    d_full = jnp.concatenate([d_full, after(d_near, parts[0])], axis=0)
    d_full = jnp.concatenate([d_full, swap(d_full, "head", 2)], axis=0)
    parts = [parts[0]] + [swap(parts[j], "slab", 8 * j) for j in (1, 2, 3)]
    d_full = after(d_full, *parts[1:])
    grad = call(grad_kernel, [((COLS, ROWS), BF)], ranks, w_out, d_full, flops=3 * 10**8, moved=3 * 10**6)[0]
    g_near = swap(grad, "slab", 8)
    att, logs = call(merge_kernel, [((COLS, ROWS), BF), ((8, ROWS), F32)], *parts, flops=10**8, moved=10**6)
    g_far = swap(jnp.concatenate([grad, after(g_near, att)], axis=0), "slab", 16)
    g_all = [grad, g_near, g_far[:COLS], g_far[COLS:]]
    stats = call(delta_kernel, [((8, ROWS), F32)], logs, att, grad, flops=10**6, moved=10**6)[0]
    stat_all = [stats] + [swap(stats, "slab", 8 * j) for j in (1, 2, 3)]
    att_other = swap(att, "slab", 1)

    mix = call(
        mix_kernel,
        [((4 * ROWS, COLS), F32), ((4 * ROWS, COLS), BF)],
        ranks,
        after(att, g_near, *stat_all[1:]),
        w_out,
        flops=3 * 10**8,
        moved=4 * 10**6,
    )
    mix_in = swap(mix[1], "head", 2)
    d_other = swap(after(d_full, g_near), "slab", 1)
    weight = call(
        weight_kernel,
        [((48, WIDE), F32)] + [((48, WIDE), BF)] * 3,
        ranks,
        att,
        att_other,
        d_full,
        d_other,
        flops=6 * 10**8,
        moved=4 * 10**6,
    )
    weight_in = [swap(weight[j], "slab", 2 * j) for j in (1, 2, 3)]
    mixed = after(mix[0], weight[1]) + mix_in.astype(F32)
    mixed_away = mixed[2 * ROWS :].astype(BF)
    mix_near = swap(mixed_away, "head", 1)
    stat_all[0] = after(stat_all[0], weight[1])

    dq_own, dq_other, own, other = call(
        backward_kernel,
        [((2 * COLS, ROWS), F32), ((2 * COLS, ROWS), BF), ((8 * ROWS, COLS), F32), ((8 * ROWS, COLS), BF)],
        ranks,
        *q_all,
        *kv_all,
        *g_all,
        *stat_all,
        flops=6 * 10**9,
        moved=6 * 10**6,
        scratch=[bias_scratch],
    )
    weight = after(weight[0], other) + sum((w.astype(F32) for w in weight_in), 0.0)
    weight_away = weight[24:].astype(BF)

    other = swap(other, "slab", 1)
    pair = (after(own, weight_away, mixed_away) + other.astype(F32)).reshape(4, 2 * ROWS, COLS)
    away = [pair[e].astype(BF) for e in (1, 2, 3)]
    arrived = [swap(away[e - 1], "slab", 2 * e) for e in (1, 2, 3)]
    weight_far = swap(weight_away, "slab", 16)
    dq_in = swap(after(dq_other, other), "slab", 16)

    mixed = after(mixed[: 2 * ROWS], arrived[1]) + mix_near.astype(F32)
    mixed_away = mixed[ROWS:].astype(BF)
    weight = after(weight[:24], mixed_away) + weight_far.astype(F32)
    weight_away = weight[12:].astype(BF)
    dq = after(dq_own, mixed_away) + dq_in.astype(F32)
    dq_away = dq[COLS:].astype(BF)

    total = after(pair[0], weight_away, mixed_away, dq_away) + sum((a.astype(F32) for a in arrived), 0.0)
    total = total.astype(BF)
    weight_grad = weight[:12] + swap(weight_away, "slab", 8).astype(F32)
    mixed = mixed[:ROWS] + swap(mixed_away, "head", 4).astype(F32)
    dq = dq[:COLS] + swap(dq_away, "slab", 8).astype(F32)
    query_grad = dq.astype(BF).T
    return mixed.astype(BF), query_grad, total[:ROWS], total[ROWS:], weight_grad


def solution(mesh):
    placed = (
        P("slab", "head"),
        P("slab", "head"),
        P("slab", "head"),
        P("head", None),
        P("slab", "head"),
        P("slab", None),
        P("slab"),
    )
    return jax.shard_map(
        on_device,
        mesh=mesh,
        in_specs=placed,
        out_specs=(
            P("slab", "head"),
            P("slab", "head"),
            P("slab", "head"),
            P("slab", "head"),
            P(("head", "slab"), None),
        ),
        check_vma=False,
    )
```

```python
import functools
import math

import jax
import jax.numpy as jnp
from jax import lax
from jax.experimental import pallas as pl
from jax.experimental.pallas import tpu as pltpu
from jax.sharding import PartitionSpec as P

HD = 128
TILE = 64
HEADS = 3
ROWS = 128
COLS = 384
WIDE = 3072
NT_DEV = 4
NY_DEV = 4
DEAD = -1e30
SCALE = 1.0 / math.sqrt(HD)
ORDER = (0, 4, 1, 5, 2, 6, 3, 7)
BF = jnp.bfloat16
F32 = jnp.float32


def swap(block, axis, distance):
    devices = range(lax.axis_size(axis))
    return lax.ppermute(block, axis, [(i, i ^ distance) for i in devices])


def dot(lhs, rhs, left, right):
    return lax.dot_general(lhs, rhs, (((left,), (right,)), ((), ())), preferred_element_type=F32)


def call(kernel, outs, *args, flops, moved, scratch=(), limit=24, by_hand=False):
    anywhere = pl.BlockSpec(memory_space=pltpu.HBM)
    vmem = pl.BlockSpec(memory_space=pltpu.VMEM)
    smem = pl.BlockSpec(memory_space=pltpu.SMEM)
    return pl.pallas_call(
        kernel,
        out_shape=[jax.ShapeDtypeStruct(shape, dtype) for shape, dtype in outs],
        in_specs=[anywhere if by_hand else smem if a.dtype == jnp.int32 else vmem for a in args],
        out_specs=[vmem] * len(outs),
        scratch_shapes=list(scratch),
        compiler_params=pltpu.CompilerParams(vmem_limit_bytes=limit * 1024 * 1024),
        cost_estimate=pl.CostEstimate(flops=1000, bytes_accessed=1000, transcendentals=0),
    )(*args)


def pack_kernel(ids_hbm, counts_hbm, q_hbm, k_hbm, v_hbm, q_out, kv_out, ids_ref, counts_ref, sems):
    copies = [
        pltpu.make_async_copy(ids_hbm, ids_ref, sems.at[0]),
        pltpu.make_async_copy(counts_hbm, counts_ref, sems.at[1]),
        pltpu.make_async_copy(k_hbm, kv_out.at[0:ROWS], sems.at[2]),
        pltpu.make_async_copy(v_hbm, kv_out.at[ROWS : 2 * ROWS], sems.at[3]),
        pltpu.make_async_copy(q_hbm, q_out.at[0:ROWS], sems.at[4]),
    ]
    for copy in copies:
        copy.start()
    copies[0].wait()
    copies[1].wait()
    row = lax.broadcasted_iota(jnp.int32, (16, COLS), 0)
    col = lax.broadcasted_iota(jnp.int32, (16, COLS), 1)
    named = jnp.full((16, COLS), -1.0, F32)
    for tile in range(2):
        for f in range(4):
            one = jnp.where(f < counts_ref[tile], ids_ref[tile, f], -1).astype(F32)
            named = jnp.where((row == tile) & (col == f), one, named)
    q_out[ROWS : ROWS + 16, :] = named.astype(BF)
    for copy in copies[2:]:
        copy.wait()


def after(value, *others):
    return lax.optimization_barrier((value, others))[0]


def log_counts(rank_ref, q_refs):
    t, y, c = rank_ref[0], rank_ref[1], rank_ref[2]
    row = lax.broadcasted_iota(jnp.int32, (16, ROWS), 0)
    lane = lax.broadcasted_iota(jnp.int32, (16, ROWS), 1)
    block = row // 2
    height = (y ^ (block % 4)) * 2 + (c ^ (block // 4))
    tile = (((t * 8 + height) * 2) + row % 2).astype(F32)
    near_height = jnp.abs(height - (y * 2 + c)) <= 1
    parts = []
    for j, q in enumerate(q_refs):
        near_time = jnp.abs((t ^ j) - t) <= 1
        count = jnp.where(near_height & near_time, 1.0, 0.0)
        named = q[ROWS : ROWS + 16, 0:HD].astype(F32)
        for f in range(4):
            one = jnp.where(lane < TILE, named[0:1, f : f + 1], named[1:2, f : f + 1])
            count = count + jnp.where(one == tile, 1.0, 0.0)
        parts.append(jnp.where(count > 0, jnp.log(jnp.maximum(count, 1.0)), DEAD))
    return jnp.concatenate(parts, axis=1)


def forward_kernel(*refs):
    rank_ref, q_refs, kv_refs = refs[0], refs[1:5], refs[5:13]
    out_refs, s_ref, bias_ref = refs[13:17], refs[17], refs[18]
    bias_ref[...] = log_counts(rank_ref, q_refs)
    row = lax.broadcasted_iota(jnp.int32, (16, 4 * ROWS), 0)
    stats = jnp.zeros((16, 4 * ROWS), F32)
    for h in range(HEADS):
        cols = slice(h * HD, (h + 1) * HD)
        q = jnp.concatenate([r[0:ROWS, cols] for r in q_refs], axis=0)
        top = jnp.full((1, 4 * ROWS), 2 * DEAD, F32)
        for b, kv in enumerate(kv_refs):
            s = dot(kv[0:ROWS, cols], q, 1, 1) * SCALE
            for half in range(2):
                part = s[half * TILE : (half + 1) * TILE] + bias_ref[2 * b + half : 2 * b + half + 1, :]
                start = b * ROWS + half * TILE
                s_ref[start : start + TILE, :] = part
                top = jnp.maximum(top, jnp.max(part, axis=0, keepdims=True))
        total = jnp.zeros((1, 4 * ROWS), F32)
        out = jnp.zeros((HD, 4 * ROWS), F32)
        for b, kv in enumerate(kv_refs):
            e = jnp.exp(s_ref[b * ROWS : (b + 1) * ROWS, :] - top)
            total = total + jnp.sum(e, axis=0, keepdims=True)
            out = out + dot(kv[ROWS : 2 * ROWS, cols], e.astype(BF), 0, 0)
        out = (out / total).astype(BF)
        for j, r in enumerate(out_refs):
            r[cols, :] = out[:, j * ROWS : (j + 1) * ROWS]
        rest = top + jnp.log(total)
        for piece in range(3):
            high = rest.astype(BF).astype(F32)
            stats = jnp.where(row == 3 * h + piece, high, stats)
            rest = rest - high
    stats = stats.astype(BF)
    for j, r in enumerate(out_refs):
        r[COLS : COLS + 16, :] = stats[:, j * ROWS : (j + 1) * ROWS]


def merge_kernel(*refs):
    parts, att_ref, logs_ref = refs[:4], refs[4], refs[5]
    row = lax.broadcasted_iota(jnp.int32, (8, ROWS), 0)
    merged = jnp.zeros((8, ROWS), F32)
    pieces = [r[COLS : COLS + 16, :].astype(F32) for r in parts]
    for h in range(HEADS):
        cols = slice(h * HD, (h + 1) * HD)
        logs = [(p[3 * h : 3 * h + 1] + p[3 * h + 1 : 3 * h + 2]) + p[3 * h + 2 : 3 * h + 3] for p in pieces]
        top = functools.reduce(jnp.maximum, logs)
        shares = [jnp.exp(l - top) for l in logs]
        total = functools.reduce(jnp.add, shares)
        out = sum((r[cols, :].astype(F32) * (w / total) for r, w in zip(parts, shares)), jnp.zeros((HD, ROWS), F32))
        att_ref[cols, :] = out.astype(BF)
        merged = jnp.where(row == h, top + jnp.log(total), merged)
    logs_ref[...] = merged


def delta_kernel(logs_ref, att_ref, grad_ref, stats_ref):
    row = lax.broadcasted_iota(jnp.int32, (8, ROWS), 0)
    stats = logs_ref[...]
    for h in range(HEADS):
        cols = slice(h * HD, (h + 1) * HD)
        delta = jnp.sum(att_ref[cols, :].astype(F32) * grad_ref[cols, :].astype(F32), axis=0, keepdims=True)
        stats = jnp.where(row == 3 + h, delta, stats)
    stats_ref[...] = stats


def grad_kernel(rank_ref, w_ref, d_ref, out_ref):
    total = jnp.zeros((COLS, ROWS), F32)
    for p in range(8):
        start = pl.multiple_of((rank_ref[3] ^ ORDER[p]) * COLS, 128)
        total = total + dot(w_ref[:, pl.ds(start, COLS)], d_ref[p * ROWS : (p + 1) * ROWS, :], 1, 1)
    out_ref[...] = total.astype(BF)


def mix_kernel(rank_ref, att_ref, w_ref, own_ref, other_ref):
    att = att_ref[...].T
    for i, p in enumerate(ORDER):
        start = pl.multiple_of((rank_ref[3] ^ p) * COLS, 128)
        part = jnp.dot(att, w_ref[:, pl.ds(start, COLS)], preferred_element_type=F32)
        target = own_ref if i < 4 else other_ref
        target[(i % 4) * ROWS : (i % 4 + 1) * ROWS, :] = part.astype(target.dtype)


def weight_kernel(rank_ref, att_ref, att2_ref, d_ref, d2_ref, own_ref, *out_refs):
    t, y, c = rank_ref[0], rank_ref[1], rank_ref[2]
    row = lax.broadcasted_iota(jnp.int32, (192, COLS), 0)
    col = lax.broadcasted_iota(jnp.int32, (192, COLS), 1)
    source = row * 0
    for jy in range(4):
        for place, jt in enumerate((0, 2, 1, 3)):
            low = jy * 48 + place * 12
            base = (t ^ jt) * 96 + (y ^ jy) * 24 + c * 12 - low
            source = jnp.where((row >= low) & (row < low + 12), row + base, source)
    pick = jnp.where(source == col, 1.0, 0.0).astype(BF)
    first = jnp.dot(pick, att_ref[...], preferred_element_type=F32).astype(BF)
    second = jnp.dot(pick, att2_ref[...], preferred_element_type=F32).astype(BF)
    both = jnp.concatenate([first, second], axis=1)
    for p in range(8):
        start = pl.multiple_of((rank_ref[3] ^ ORDER[p]) * COLS, 128)
        rows = slice(p * ROWS, (p + 1) * ROWS)
        rhs = jnp.concatenate([d_ref[rows, :], d2_ref[rows, :]], axis=0)
        part = jnp.dot(both, rhs, preferred_element_type=F32)
        own_ref[:, pl.ds(start, COLS)] = part[0:48]
        for j in range(3):
            out_refs[j][:, pl.ds(start, COLS)] = part[48 * (j + 1) : 48 * (j + 2)].astype(BF)


def backward_kernel(*refs):
    rank_ref, q_refs, kv_refs = refs[0], refs[1:5], refs[5:13]
    g_refs, stat_refs = refs[13:17], refs[17:21]
    dq_own, dq_other, own_ref, other_ref, bias_ref = refs[21:26]
    bias_ref[...] = log_counts(rank_ref, q_refs)
    for h in range(HEADS):
        cols = slice(h * HD, (h + 1) * HD)
        q = jnp.concatenate([r[0:ROWS, cols] for r in q_refs], axis=0)
        g = jnp.concatenate([r[cols, :] for r in g_refs], axis=1)
        log_total = jnp.concatenate([r[h : h + 1, :] for r in stat_refs], axis=1)
        delta = jnp.concatenate([r[3 + h : 4 + h, :] for r in stat_refs], axis=1)
        dq = jnp.zeros((HD, 4 * ROWS), F32)
        for b, kv in enumerate(kv_refs):
            k, v = kv[0:ROWS, cols], kv[ROWS : 2 * ROWS, cols]
            s = dot(k, q, 1, 1) * SCALE
            bias = [
                jnp.broadcast_to(bias_ref[2 * b + half : 2 * b + half + 1, :], (TILE, 4 * ROWS)) for half in range(2)
            ]
            p = jnp.exp(s + jnp.concatenate(bias, axis=0) - log_total)
            ds = (p * (jnp.dot(v, g, preferred_element_type=F32) - delta)).astype(BF)
            dv = dot(p.astype(BF), g, 1, 1)
            dk = jnp.dot(ds, q, preferred_element_type=F32) * SCALE
            dq = dq + dot(k, ds, 0, 0)
            place = (b % 4) * 2 * ROWS
            target = own_ref if b < 4 else other_ref
            target[place : place + ROWS, cols] = dk.astype(target.dtype)
            target[place + ROWS : place + 2 * ROWS, cols] = dv.astype(target.dtype)
        dq = dq * SCALE
        for j in range(4):
            target = dq_other if j % 2 else dq_own
            start = (j // 2) * COLS + h * HD
            target[start : start + HD, :] = dq[:, j * ROWS : (j + 1) * ROWS].astype(target.dtype)


def on_device(queries, keys, values, w_out, d_out, far_ids, far_counts):
    slab = lax.axis_index("slab")
    head = lax.axis_index("head")
    t, y, c = slab // 8, slab // 2 % 4, slab % 2
    ranks = jnp.stack([t, y, c, head]).astype(jnp.int32)

    q_ext, kv = call(
        pack_kernel,
        [((ROWS + 16, COLS), BF), ((2 * ROWS, COLS), BF)],
        far_ids,
        far_counts,
        queries,
        keys,
        values,
        flops=0,
        moved=10**6,
        scratch=[pltpu.SMEM((2, 4), jnp.int32), pltpu.SMEM((2,), jnp.int32), pltpu.SemaphoreType.DMA((5,))],
        by_hand=True,
        limit=58,
    )
    kv_near = [kv] + [swap(kv, "slab", 2 * e) for e in (1, 2, 3)]
    q_all = [q_ext] + [swap(q_ext, "slab", 8 * j) for j in (1, 2, 3)]
    kv_all = kv_near + [swap(block, "slab", 1) for block in kv_near]

    d_across = after(swap(after(d_out, q_all[1]), "head", 4), *kv_near, *q_all)
    d_full = jnp.concatenate([d_out, d_across], axis=0)
    d_near = swap(d_full, "head", 1)

    bias_scratch = pltpu.VMEM((16, 4 * ROWS), F32)
    parts = call(
        forward_kernel,
        [((COLS + 16, ROWS), BF)] * 4,
        ranks,
        *q_all,
        *kv_all,
        flops=3 * 10**9,
        moved=3 * 10**6,
        scratch=[pltpu.VMEM((8 * ROWS, 4 * ROWS), F32), bias_scratch],
    )
    d_full = jnp.concatenate([d_full, after(d_near, parts[0])], axis=0)
    d_full = jnp.concatenate([d_full, swap(d_full, "head", 2)], axis=0)
    parts = [parts[0]] + [swap(parts[j], "slab", 8 * j) for j in (1, 2, 3)]
    d_full = after(d_full, *parts[1:])
    grad = call(grad_kernel, [((COLS, ROWS), BF)], ranks, w_out, d_full, flops=3 * 10**8, moved=3 * 10**6)[0]
    g_near = swap(grad, "slab", 16)
    att, logs = call(merge_kernel, [((COLS, ROWS), BF), ((8, ROWS), F32)], *parts, flops=10**8, moved=10**6)
    stats = call(delta_kernel, [((8, ROWS), F32)], logs, att, grad, flops=10**6, moved=10**6)[0]
    stat_all = [stats] + [swap(stats, "slab", 8 * j) for j in (1, 2, 3)]
    att_other = swap(att, "slab", 1)

    mix = call(
        mix_kernel,
        [((4 * ROWS, COLS), F32), ((4 * ROWS, COLS), BF)],
        ranks,
        after(att, grad),
        w_out,
        flops=3 * 10**8,
        moved=4 * 10**6,
    )
    mix_in = swap(mix[1], "head", 2)
    g_far = swap(jnp.concatenate([grad, after(g_near, mix[1])], axis=0), "slab", 8)
    g_all = [grad, g_far[:COLS], g_near, g_far[COLS:]]
    d_other = swap(after(d_full, att), "slab", 1)
    weight = call(
        weight_kernel,
        [((48, WIDE), F32)] + [((48, WIDE), BF)] * 3,
        ranks,
        att,
        att_other,
        d_full,
        d_other,
        flops=6 * 10**8,
        moved=4 * 10**6,
    )
    weight_in = [swap(weight[j], "slab", 2 * j) for j in (1, 2, 3)]
    mixed = mix[0] + mix_in.astype(F32)
    mixed_away = mixed[2 * ROWS :].astype(BF)
    stat_all[0] = after(stat_all[0], weight[1], mixed_away)

    dq_own, dq_other, own, other = call(
        backward_kernel,
        [((2 * COLS, ROWS), F32), ((2 * COLS, ROWS), BF), ((8 * ROWS, COLS), F32), ((8 * ROWS, COLS), BF)],
        ranks,
        *q_all,
        *kv_all,
        *g_all,
        *stat_all,
        flops=6 * 10**9,
        moved=6 * 10**6,
        scratch=[bias_scratch],
    )
    weight = after(weight[0], other) + sum((w.astype(F32) for w in weight_in), 0.0)
    weight_away = weight[24:].astype(BF)

    other = swap(other, "slab", 1)
    pair = (after(own, weight_away) + other.astype(F32)).reshape(4, 2 * ROWS, COLS)
    away = [pair[e].astype(BF) for e in (1, 2, 3)]
    arrived = [swap(away[e - 1], "slab", 2 * e) for e in (1, 2, 3)]
    dq_in = swap(after(dq_other, other), "slab", 8)

    mixed = after(mixed[: 2 * ROWS], arrived[1]) + swap(mixed_away, "head", 1).astype(F32)
    mixed_away = mixed[ROWS:].astype(BF)
    weight = after(weight[:24], mixed_away) + swap(weight_away, "slab", 8).astype(F32)
    weight_away = weight[12:].astype(BF)
    dq = after(dq_own, mixed_away) + dq_in.astype(F32)
    dq_away = dq[COLS:].astype(BF)

    total = after(pair[0], weight_away, mixed_away, dq_away) + sum((a.astype(F32) for a in arrived), 0.0)
    total = total.astype(BF)
    weight_grad = weight[:12] + swap(weight_away, "slab", 16).astype(F32)
    mixed = mixed[:ROWS] + swap(mixed_away, "head", 4).astype(F32)
    dq = dq[:COLS] + swap(dq_away, "slab", 16).astype(F32)
    query_grad = dq.astype(BF).T
    return mixed.astype(BF), query_grad, total[:ROWS], total[ROWS:], weight_grad


def solution(mesh):
    placed = (
        P("slab", "head"),
        P("slab", "head"),
        P("slab", "head"),
        P("head", None),
        P("slab", "head"),
        P("slab", None),
        P("slab"),
    )
    return jax.shard_map(
        on_device,
        mesh=mesh,
        in_specs=placed,
        out_specs=(
            P("slab", "head"),
            P("slab", "head"),
            P("slab", "head"),
            P("slab", "head"),
            P(("head", "slab"), None),
        ),
        check_vma=False,
    )
```

```python
import functools
import math

import jax
import jax.numpy as jnp
from jax import lax
from jax.experimental import pallas as pl
from jax.experimental.pallas import tpu as pltpu
from jax.sharding import PartitionSpec as P

HD = 128
TILE = 64
HEADS = 3
ROWS = 128
COLS = 384
WIDE = 3072
NT_DEV = 4
NY_DEV = 4
DEAD = -1e30
SCALE = 1.0 / math.sqrt(HD)
ORDER = (0, 4, 1, 5, 2, 6, 3, 7)
BF = jnp.bfloat16
F32 = jnp.float32


def swap(block, axis, distance):
    devices = range(lax.axis_size(axis))
    return lax.ppermute(block, axis, [(i, i ^ distance) for i in devices])


def dot(lhs, rhs, left, right):
    return lax.dot_general(lhs, rhs, (((left,), (right,)), ((), ())), preferred_element_type=F32)


def call(kernel, outs, *args, flops, moved, scratch=(), limit=24, by_hand=False):
    anywhere = pl.BlockSpec(memory_space=pltpu.HBM)
    vmem = pl.BlockSpec(memory_space=pltpu.VMEM)
    smem = pl.BlockSpec(memory_space=pltpu.SMEM)
    return pl.pallas_call(
        kernel,
        out_shape=[jax.ShapeDtypeStruct(shape, dtype) for shape, dtype in outs],
        in_specs=[anywhere if by_hand else smem if a.dtype == jnp.int32 else vmem for a in args],
        out_specs=[vmem] * len(outs),
        scratch_shapes=list(scratch),
        compiler_params=pltpu.CompilerParams(vmem_limit_bytes=limit * 1024 * 1024),
        cost_estimate=pl.CostEstimate(flops=1000, bytes_accessed=1000, transcendentals=0),
    )(*args)


def pack_kernel(ids_hbm, counts_hbm, q_hbm, k_hbm, v_hbm, q_out, kv_out, ids_ref, counts_ref, sems):
    copies = [
        pltpu.make_async_copy(ids_hbm, ids_ref, sems.at[0]),
        pltpu.make_async_copy(counts_hbm, counts_ref, sems.at[1]),
        pltpu.make_async_copy(k_hbm, kv_out.at[0:ROWS], sems.at[2]),
        pltpu.make_async_copy(v_hbm, kv_out.at[ROWS : 2 * ROWS], sems.at[3]),
        pltpu.make_async_copy(q_hbm, q_out.at[0:ROWS], sems.at[4]),
    ]
    for copy in copies:
        copy.start()
    copies[0].wait()
    copies[1].wait()
    row = lax.broadcasted_iota(jnp.int32, (16, COLS), 0)
    col = lax.broadcasted_iota(jnp.int32, (16, COLS), 1)
    named = jnp.full((16, COLS), -1.0, F32)
    for tile in range(2):
        for f in range(4):
            one = jnp.where(f < counts_ref[tile], ids_ref[tile, f], -1).astype(F32)
            named = jnp.where((row == tile) & (col == f), one, named)
    q_out[ROWS : ROWS + 16, :] = named.astype(BF)
    for copy in copies[2:]:
        copy.wait()


def after(value, *others):
    return lax.optimization_barrier((value, others))[0]


def log_counts(rank_ref, q_refs):
    t, y, c = rank_ref[0], rank_ref[1], rank_ref[2]
    row = lax.broadcasted_iota(jnp.int32, (16, ROWS), 0)
    lane = lax.broadcasted_iota(jnp.int32, (16, ROWS), 1)
    block = row // 2
    height = (y ^ (block % 4)) * 2 + (c ^ (block // 4))
    tile = (((t * 8 + height) * 2) + row % 2).astype(F32)
    near_height = jnp.abs(height - (y * 2 + c)) <= 1
    parts = []
    for j, q in enumerate(q_refs):
        near_time = jnp.abs((t ^ j) - t) <= 1
        count = jnp.where(near_height & near_time, 1.0, 0.0)
        named = q[ROWS : ROWS + 16, 0:HD].astype(F32)
        for f in range(4):
            one = jnp.where(lane < TILE, named[0:1, f : f + 1], named[1:2, f : f + 1])
            count = count + jnp.where(one == tile, 1.0, 0.0)
        parts.append(jnp.where(count > 0, jnp.log(jnp.maximum(count, 1.0)), DEAD))
    return jnp.concatenate(parts, axis=1)


def forward_kernel(*refs):
    rank_ref, q_refs, kv_refs = refs[0], refs[1:5], refs[5:13]
    out_refs, s_ref, bias_ref = refs[13:17], refs[17], refs[18]
    bias_ref[...] = log_counts(rank_ref, q_refs)
    row = lax.broadcasted_iota(jnp.int32, (16, 4 * ROWS), 0)
    stats = jnp.zeros((16, 4 * ROWS), F32)
    for h in range(HEADS):
        cols = slice(h * HD, (h + 1) * HD)
        q = jnp.concatenate([r[0:ROWS, cols] for r in q_refs], axis=0)
        top = jnp.full((1, 4 * ROWS), 2 * DEAD, F32)
        for b, kv in enumerate(kv_refs):
            s = dot(kv[0:ROWS, cols], q, 1, 1) * SCALE
            for half in range(2):
                part = s[half * TILE : (half + 1) * TILE] + bias_ref[2 * b + half : 2 * b + half + 1, :]
                start = b * ROWS + half * TILE
                s_ref[start : start + TILE, :] = part
                top = jnp.maximum(top, jnp.max(part, axis=0, keepdims=True))
        total = jnp.zeros((1, 4 * ROWS), F32)
        out = jnp.zeros((HD, 4 * ROWS), F32)
        for b, kv in enumerate(kv_refs):
            e = jnp.exp(s_ref[b * ROWS : (b + 1) * ROWS, :] - top)
            total = total + jnp.sum(e, axis=0, keepdims=True)
            out = out + dot(kv[ROWS : 2 * ROWS, cols], e.astype(BF), 0, 0)
        out = (out / total).astype(BF)
        for j, r in enumerate(out_refs):
            r[cols, :] = out[:, j * ROWS : (j + 1) * ROWS]
        rest = top + jnp.log(total)
        for piece in range(3):
            high = rest.astype(BF).astype(F32)
            stats = jnp.where(row == 3 * h + piece, high, stats)
            rest = rest - high
    stats = stats.astype(BF)
    for j, r in enumerate(out_refs):
        r[COLS : COLS + 16, :] = stats[:, j * ROWS : (j + 1) * ROWS]


def merge_kernel(*refs):
    parts, att_ref, logs_ref = refs[:4], refs[4], refs[5]
    row = lax.broadcasted_iota(jnp.int32, (8, ROWS), 0)
    merged = jnp.zeros((8, ROWS), F32)
    pieces = [r[COLS : COLS + 16, :].astype(F32) for r in parts]
    for h in range(HEADS):
        cols = slice(h * HD, (h + 1) * HD)
        logs = [(p[3 * h : 3 * h + 1] + p[3 * h + 1 : 3 * h + 2]) + p[3 * h + 2 : 3 * h + 3] for p in pieces]
        top = functools.reduce(jnp.maximum, logs)
        shares = [jnp.exp(l - top) for l in logs]
        total = functools.reduce(jnp.add, shares)
        out = sum((r[cols, :].astype(F32) * (w / total) for r, w in zip(parts, shares)), jnp.zeros((HD, ROWS), F32))
        att_ref[cols, :] = out.astype(BF)
        merged = jnp.where(row == h, top + jnp.log(total), merged)
    logs_ref[...] = merged


def delta_kernel(logs_ref, att_ref, grad_ref, stats_ref):
    row = lax.broadcasted_iota(jnp.int32, (8, ROWS), 0)
    stats = logs_ref[...]
    for h in range(HEADS):
        cols = slice(h * HD, (h + 1) * HD)
        delta = jnp.sum(att_ref[cols, :].astype(F32) * grad_ref[cols, :].astype(F32), axis=0, keepdims=True)
        stats = jnp.where(row == 3 + h, delta, stats)
    stats_ref[...] = stats


def grad_kernel(rank_ref, w_ref, d_ref, out_ref):
    total = jnp.zeros((COLS, ROWS), F32)
    for p in range(8):
        start = pl.multiple_of((rank_ref[3] ^ ORDER[p]) * COLS, 128)
        total = total + dot(w_ref[:, pl.ds(start, COLS)], d_ref[p * ROWS : (p + 1) * ROWS, :], 1, 1)
    out_ref[...] = total.astype(BF)


def mix_kernel(rank_ref, att_ref, w_ref, own_ref, other_ref):
    att = att_ref[...].T
    for i, p in enumerate(ORDER):
        start = pl.multiple_of((rank_ref[3] ^ p) * COLS, 128)
        part = jnp.dot(att, w_ref[:, pl.ds(start, COLS)], preferred_element_type=F32)
        target = own_ref if i < 4 else other_ref
        target[(i % 4) * ROWS : (i % 4 + 1) * ROWS, :] = part.astype(target.dtype)


def weight_kernel(rank_ref, att_ref, att2_ref, d_ref, d2_ref, own_ref, *out_refs):
    t, y, c = rank_ref[0], rank_ref[1], rank_ref[2]
    row = lax.broadcasted_iota(jnp.int32, (192, COLS), 0)
    col = lax.broadcasted_iota(jnp.int32, (192, COLS), 1)
    source = row * 0
    for jy in range(4):
        for place, jt in enumerate((0, 2, 1, 3)):
            low = jy * 48 + place * 12
            base = (t ^ jt) * 96 + (y ^ jy) * 24 + c * 12 - low
            source = jnp.where((row >= low) & (row < low + 12), row + base, source)
    pick = jnp.where(source == col, 1.0, 0.0).astype(BF)
    first = jnp.dot(pick, att_ref[...], preferred_element_type=F32).astype(BF)
    second = jnp.dot(pick, att2_ref[...], preferred_element_type=F32).astype(BF)
    both = jnp.concatenate([first, second], axis=1)
    for p in range(8):
        start = pl.multiple_of((rank_ref[3] ^ ORDER[p]) * COLS, 128)
        rows = slice(p * ROWS, (p + 1) * ROWS)
        rhs = jnp.concatenate([d_ref[rows, :], d2_ref[rows, :]], axis=0)
        part = jnp.dot(both, rhs, preferred_element_type=F32)
        own_ref[:, pl.ds(start, COLS)] = part[0:48]
        for j in range(3):
            out_refs[j][:, pl.ds(start, COLS)] = part[48 * (j + 1) : 48 * (j + 2)].astype(BF)


def backward_kernel(*refs):
    rank_ref, q_refs, kv_refs = refs[0], refs[1:5], refs[5:13]
    g_refs, stat_refs = refs[13:17], refs[17:21]
    dq_own, dq_other, own_ref, other_ref, bias_ref = refs[21:26]
    bias_ref[...] = log_counts(rank_ref, q_refs)
    for h in range(HEADS):
        cols = slice(h * HD, (h + 1) * HD)
        q = jnp.concatenate([r[0:ROWS, cols] for r in q_refs], axis=0)
        g = jnp.concatenate([r[cols, :] for r in g_refs], axis=1)
        log_total = jnp.concatenate([r[h : h + 1, :] for r in stat_refs], axis=1)
        delta = jnp.concatenate([r[3 + h : 4 + h, :] for r in stat_refs], axis=1)
        dq = jnp.zeros((HD, 4 * ROWS), F32)
        for b, kv in enumerate(kv_refs):
            k, v = kv[0:ROWS, cols], kv[ROWS : 2 * ROWS, cols]
            s = dot(k, q, 1, 1) * SCALE
            bias = [
                jnp.broadcast_to(bias_ref[2 * b + half : 2 * b + half + 1, :], (TILE, 4 * ROWS)) for half in range(2)
            ]
            p = jnp.exp(s + jnp.concatenate(bias, axis=0) - log_total)
            ds = (p * (jnp.dot(v, g, preferred_element_type=F32) - delta)).astype(BF)
            dv = dot(p.astype(BF), g, 1, 1)
            dk = jnp.dot(ds, q, preferred_element_type=F32) * SCALE
            dq = dq + dot(k, ds, 0, 0)
            place = (b % 4) * 2 * ROWS
            target = own_ref if b < 4 else other_ref
            target[place : place + ROWS, cols] = dk.astype(target.dtype)
            target[place + ROWS : place + 2 * ROWS, cols] = dv.astype(target.dtype)
        dq = dq * SCALE
        for j in range(4):
            target = dq_other if j % 2 else dq_own
            start = (j // 2) * COLS + h * HD
            target[start : start + HD, :] = dq[:, j * ROWS : (j + 1) * ROWS].astype(target.dtype)


def on_device(queries, keys, values, w_out, d_out, far_ids, far_counts):
    slab = lax.axis_index("slab")
    head = lax.axis_index("head")
    t, y, c = slab // 8, slab // 2 % 4, slab % 2
    ranks = jnp.stack([t, y, c, head]).astype(jnp.int32)

    q_ext, kv = call(
        pack_kernel,
        [((ROWS + 16, COLS), BF), ((2 * ROWS, COLS), BF)],
        far_ids,
        far_counts,
        queries,
        keys,
        values,
        flops=0,
        moved=10**6,
        scratch=[pltpu.SMEM((2, 4), jnp.int32), pltpu.SMEM((2,), jnp.int32), pltpu.SemaphoreType.DMA((5,))],
        by_hand=True,
        limit=58,
    )
    kv_near = [kv] + [swap(kv, "slab", 2 * e) for e in (1, 2, 3)]
    q_all = [q_ext] + [swap(q_ext, "slab", 8 * j) for j in (1, 2, 3)]
    kv_all = kv_near + [swap(block, "slab", 1) for block in kv_near]

    d_across = after(swap(after(d_out, q_all[1]), "head", 4), *kv_near, *q_all)
    d_full = jnp.concatenate([d_out, d_across], axis=0)
    d_near = swap(d_full, "head", 1)

    bias_scratch = pltpu.VMEM((16, 4 * ROWS), F32)
    parts = call(
        forward_kernel,
        [((COLS + 16, ROWS), BF)] * 4,
        ranks,
        *q_all,
        *kv_all,
        flops=3 * 10**9,
        moved=3 * 10**6,
        scratch=[pltpu.VMEM((8 * ROWS, 4 * ROWS), F32), bias_scratch],
    )
    d_full = jnp.concatenate([d_full, after(d_near, parts[0])], axis=0)
    d_full = jnp.concatenate([d_full, swap(d_full, "head", 2)], axis=0)
    parts = [parts[0]] + [swap(parts[j], "slab", 8 * j) for j in (1, 2, 3)]
    d_full = after(d_full, *parts[1:])
    grad = call(grad_kernel, [((COLS, ROWS), BF)], ranks, w_out, d_full, flops=3 * 10**8, moved=3 * 10**6)[0]
    g_near = swap(grad, "slab", 16)
    att, logs = call(merge_kernel, [((COLS, ROWS), BF), ((8, ROWS), F32)], *parts, flops=10**8, moved=10**6)
    stats = call(delta_kernel, [((8, ROWS), F32)], logs, att, grad, flops=10**6, moved=10**6)[0]
    stat_all = [stats] + [swap(stats, "slab", 8 * j) for j in (1, 2, 3)]
    att_other = swap(att, "slab", 1)

    g_far = swap(jnp.concatenate([grad, after(g_near, *stat_all[1:], att_other)], axis=0), "slab", 8)
    d_other = swap(after(d_full, att), "slab", 1)
    weight = call(
        weight_kernel,
        [((48, WIDE), F32)] + [((48, WIDE), BF)] * 3,
        ranks,
        att,
        att_other,
        d_full,
        d_other,
        flops=6 * 10**8,
        moved=4 * 10**6,
    )
    weight_in = [swap(weight[j], "slab", 2 * j) for j in (1, 2, 3)]
    mix = call(
        mix_kernel,
        [((4 * ROWS, COLS), F32), ((4 * ROWS, COLS), BF)],
        ranks,
        after(att, weight[1]),
        w_out,
        flops=3 * 10**8,
        moved=4 * 10**6,
    )
    mix_in = swap(mix[1], "head", 2)
    g_far = after(g_far, weight[1])
    g_all = [grad, g_far[:COLS], g_near, g_far[COLS:]]
    mixed = mix[0] + mix_in.astype(F32)
    mixed_away = mixed[2 * ROWS :].astype(BF)
    stat_all[0] = after(stat_all[0], weight[1], mix[1])

    dq_own, dq_other, own, other = call(
        backward_kernel,
        [((2 * COLS, ROWS), F32), ((2 * COLS, ROWS), BF), ((8 * ROWS, COLS), F32), ((8 * ROWS, COLS), BF)],
        ranks,
        *q_all,
        *kv_all,
        *g_all,
        *stat_all,
        flops=6 * 10**9,
        moved=6 * 10**6,
        scratch=[bias_scratch],
    )
    weight = after(weight[0], other) + sum((w.astype(F32) for w in weight_in), 0.0)
    weight_away = weight[24:].astype(BF)

    other = swap(other, "slab", 1)
    pair = (after(own, weight_away, mixed_away) + other.astype(F32)).reshape(4, 2 * ROWS, COLS)
    away = [pair[e].astype(BF) for e in (1, 2, 3)]
    arrived = [swap(away[e - 1], "slab", 2 * e) for e in (1, 2, 3)]
    dq_in = swap(after(dq_other, other), "slab", 8)

    mixed = after(mixed[: 2 * ROWS], arrived[1]) + swap(mixed_away, "head", 1).astype(F32)
    mixed_away = mixed[ROWS:].astype(BF)
    weight = after(weight[:24], arrived[1]) + swap(weight_away, "slab", 8).astype(F32)
    weight_away = weight[12:].astype(BF)
    dq = after(dq_own, mixed_away) + dq_in.astype(F32)
    dq_away = dq[COLS:].astype(BF)

    total = after(pair[0], weight_away, mixed_away, dq_away) + sum((a.astype(F32) for a in arrived), 0.0)
    total = total.astype(BF)
    weight_grad = weight[:12] + swap(weight_away, "slab", 16).astype(F32)
    mixed = mixed[:ROWS] + swap(mixed_away, "head", 4).astype(F32)
    dq = dq[:COLS] + swap(dq_away, "slab", 16).astype(F32)
    query_grad = dq.astype(BF).T
    return mixed.astype(BF), query_grad, total[:ROWS], total[ROWS:], weight_grad


def solution(mesh):
    placed = (
        P("slab", "head"),
        P("slab", "head"),
        P("slab", "head"),
        P("head", None),
        P("slab", "head"),
        P("slab", None),
        P("slab"),
    )
    return jax.shard_map(
        on_device,
        mesh=mesh,
        in_specs=placed,
        out_specs=(
            P("slab", "head"),
            P("slab", "head"),
            P("slab", "head"),
            P("slab", "head"),
            P(("head", "slab"), None),
        ),
        check_vma=False,
    )
```

```python
import functools
import math

import jax
import jax.numpy as jnp
from jax import lax
from jax.experimental import pallas as pl
from jax.experimental.pallas import tpu as pltpu
from jax.sharding import PartitionSpec as P

HD = 128
TILE = 64
HEADS = 3
ROWS = 128
COLS = 384
WIDE = 3072
NT_DEV = 4
NY_DEV = 4
DEAD = -1e30
SCALE = 1.0 / math.sqrt(HD)
ORDER = (0, 4, 1, 5, 2, 6, 3, 7)
BF = jnp.bfloat16
F32 = jnp.float32


def swap(block, axis, distance):
    devices = range(lax.axis_size(axis))
    return lax.ppermute(block, axis, [(i, i ^ distance) for i in devices])


def dot(lhs, rhs, left, right):
    return lax.dot_general(lhs, rhs, (((left,), (right,)), ((), ())), preferred_element_type=F32)


def call(kernel, outs, *args, flops, moved, scratch=(), limit=24, by_hand=False):
    anywhere = pl.BlockSpec(memory_space=pltpu.HBM)
    vmem = pl.BlockSpec(memory_space=pltpu.VMEM)
    smem = pl.BlockSpec(memory_space=pltpu.SMEM)
    return pl.pallas_call(
        kernel,
        out_shape=[jax.ShapeDtypeStruct(shape, dtype) for shape, dtype in outs],
        in_specs=[anywhere if by_hand else smem if a.dtype == jnp.int32 else vmem for a in args],
        out_specs=[vmem] * len(outs),
        scratch_shapes=list(scratch),
        compiler_params=pltpu.CompilerParams(vmem_limit_bytes=limit * 1024 * 1024),
        cost_estimate=pl.CostEstimate(flops=1000, bytes_accessed=1000, transcendentals=0),
    )(*args)


def pack_kernel(ids_hbm, counts_hbm, q_hbm, k_hbm, v_hbm, q_out, kv_out, ids_ref, counts_ref, sems):
    copies = [
        pltpu.make_async_copy(ids_hbm, ids_ref, sems.at[0]),
        pltpu.make_async_copy(counts_hbm, counts_ref, sems.at[1]),
        pltpu.make_async_copy(k_hbm, kv_out.at[0:ROWS], sems.at[2]),
        pltpu.make_async_copy(v_hbm, kv_out.at[ROWS : 2 * ROWS], sems.at[3]),
        pltpu.make_async_copy(q_hbm, q_out.at[0:ROWS], sems.at[4]),
    ]
    for copy in copies:
        copy.start()
    copies[0].wait()
    copies[1].wait()
    row = lax.broadcasted_iota(jnp.int32, (16, COLS), 0)
    col = lax.broadcasted_iota(jnp.int32, (16, COLS), 1)
    named = jnp.full((16, COLS), -1.0, F32)
    for tile in range(2):
        for f in range(4):
            one = jnp.where(f < counts_ref[tile], ids_ref[tile, f], -1).astype(F32)
            named = jnp.where((row == tile) & (col == f), one, named)
    q_out[ROWS : ROWS + 16, :] = named.astype(BF)
    for copy in copies[2:]:
        copy.wait()


def after(value, *others):
    return lax.optimization_barrier((value, others))[0]


def log_counts(rank_ref, q_refs):
    t, y, c = rank_ref[0], rank_ref[1], rank_ref[2]
    row = lax.broadcasted_iota(jnp.int32, (16, ROWS), 0)
    lane = lax.broadcasted_iota(jnp.int32, (16, ROWS), 1)
    block = row // 2
    height = (y ^ (block % 4)) * 2 + (c ^ (block // 4))
    tile = (((t * 8 + height) * 2) + row % 2).astype(F32)
    near_height = jnp.abs(height - (y * 2 + c)) <= 1
    parts = []
    for j, q in enumerate(q_refs):
        near_time = jnp.abs((t ^ j) - t) <= 1
        count = jnp.where(near_height & near_time, 1.0, 0.0)
        named = q[ROWS : ROWS + 16, 0:HD].astype(F32)
        for f in range(4):
            one = jnp.where(lane < TILE, named[0:1, f : f + 1], named[1:2, f : f + 1])
            count = count + jnp.where(one == tile, 1.0, 0.0)
        parts.append(jnp.where(count > 0, jnp.log(jnp.maximum(count, 1.0)), DEAD))
    return jnp.concatenate(parts, axis=1)


def forward_kernel(*refs):
    rank_ref, q_refs, kv_refs = refs[0], refs[1:5], refs[5:13]
    out_refs, s_ref, bias_ref = refs[13:17], refs[17], refs[18]
    bias_ref[...] = log_counts(rank_ref, q_refs)
    row = lax.broadcasted_iota(jnp.int32, (16, 4 * ROWS), 0)
    stats = jnp.zeros((16, 4 * ROWS), F32)
    for h in range(HEADS):
        cols = slice(h * HD, (h + 1) * HD)
        q = jnp.concatenate([r[0:ROWS, cols] for r in q_refs], axis=0)
        top = jnp.full((1, 4 * ROWS), 2 * DEAD, F32)
        for b, kv in enumerate(kv_refs):
            s = dot(kv[0:ROWS, cols], q, 1, 1) * SCALE
            for half in range(2):
                part = s[half * TILE : (half + 1) * TILE] + bias_ref[2 * b + half : 2 * b + half + 1, :]
                start = b * ROWS + half * TILE
                s_ref[start : start + TILE, :] = part
                top = jnp.maximum(top, jnp.max(part, axis=0, keepdims=True))
        total = jnp.zeros((1, 4 * ROWS), F32)
        out = jnp.zeros((HD, 4 * ROWS), F32)
        for b, kv in enumerate(kv_refs):
            e = jnp.exp(s_ref[b * ROWS : (b + 1) * ROWS, :] - top)
            total = total + jnp.sum(e, axis=0, keepdims=True)
            out = out + dot(kv[ROWS : 2 * ROWS, cols], e.astype(BF), 0, 0)
        out = (out / total).astype(BF)
        for j, r in enumerate(out_refs):
            r[cols, :] = out[:, j * ROWS : (j + 1) * ROWS]
        rest = top + jnp.log(total)
        for piece in range(3):
            high = rest.astype(BF).astype(F32)
            stats = jnp.where(row == 3 * h + piece, high, stats)
            rest = rest - high
    stats = stats.astype(BF)
    for j, r in enumerate(out_refs):
        r[COLS : COLS + 16, :] = stats[:, j * ROWS : (j + 1) * ROWS]


def merge_kernel(*refs):
    parts, att_ref, logs_ref = refs[:4], refs[4], refs[5]
    row = lax.broadcasted_iota(jnp.int32, (8, ROWS), 0)
    merged = jnp.zeros((8, ROWS), F32)
    pieces = [r[COLS : COLS + 16, :].astype(F32) for r in parts]
    for h in range(HEADS):
        cols = slice(h * HD, (h + 1) * HD)
        logs = [(p[3 * h : 3 * h + 1] + p[3 * h + 1 : 3 * h + 2]) + p[3 * h + 2 : 3 * h + 3] for p in pieces]
        top = functools.reduce(jnp.maximum, logs)
        shares = [jnp.exp(l - top) for l in logs]
        total = functools.reduce(jnp.add, shares)
        out = sum((r[cols, :].astype(F32) * (w / total) for r, w in zip(parts, shares)), jnp.zeros((HD, ROWS), F32))
        att_ref[cols, :] = out.astype(BF)
        merged = jnp.where(row == h, top + jnp.log(total), merged)
    logs_ref[...] = merged


def delta_kernel(logs_ref, att_ref, grad_ref, stats_ref):
    row = lax.broadcasted_iota(jnp.int32, (8, ROWS), 0)
    stats = logs_ref[...]
    for h in range(HEADS):
        cols = slice(h * HD, (h + 1) * HD)
        delta = jnp.sum(att_ref[cols, :].astype(F32) * grad_ref[cols, :].astype(F32), axis=0, keepdims=True)
        stats = jnp.where(row == 3 + h, delta, stats)
    stats_ref[...] = stats


def grad_kernel(rank_ref, w_ref, d_ref, out_ref):
    total = jnp.zeros((COLS, ROWS), F32)
    for p in range(8):
        start = pl.multiple_of((rank_ref[3] ^ ORDER[p]) * COLS, 128)
        total = total + dot(w_ref[:, pl.ds(start, COLS)], d_ref[p * ROWS : (p + 1) * ROWS, :], 1, 1)
    out_ref[...] = total.astype(BF)


def mix_kernel(rank_ref, att_ref, w_ref, own_ref, other_ref):
    att = att_ref[...].T
    for i, p in enumerate(ORDER):
        start = pl.multiple_of((rank_ref[3] ^ p) * COLS, 128)
        part = jnp.dot(att, w_ref[:, pl.ds(start, COLS)], preferred_element_type=F32)
        target = own_ref if i < 4 else other_ref
        target[(i % 4) * ROWS : (i % 4 + 1) * ROWS, :] = part.astype(target.dtype)


def weight_kernel(rank_ref, att_ref, att2_ref, d_ref, d2_ref, own_ref, *out_refs):
    t, y, c = rank_ref[0], rank_ref[1], rank_ref[2]
    row = lax.broadcasted_iota(jnp.int32, (192, COLS), 0)
    col = lax.broadcasted_iota(jnp.int32, (192, COLS), 1)
    source = row * 0
    for jy in range(4):
        for place, jt in enumerate((0, 2, 1, 3)):
            low = jy * 48 + place * 12
            base = (t ^ jt) * 96 + (y ^ jy) * 24 + c * 12 - low
            source = jnp.where((row >= low) & (row < low + 12), row + base, source)
    pick = jnp.where(source == col, 1.0, 0.0).astype(BF)
    first = jnp.dot(pick, att_ref[...], preferred_element_type=F32).astype(BF)
    second = jnp.dot(pick, att2_ref[...], preferred_element_type=F32).astype(BF)
    both = jnp.concatenate([first, second], axis=1)
    for p in range(8):
        start = pl.multiple_of((rank_ref[3] ^ ORDER[p]) * COLS, 128)
        rows = slice(p * ROWS, (p + 1) * ROWS)
        rhs = jnp.concatenate([d_ref[rows, :], d2_ref[rows, :]], axis=0)
        part = jnp.dot(both, rhs, preferred_element_type=F32)
        own_ref[:, pl.ds(start, COLS)] = part[0:48]
        for j in range(3):
            out_refs[j][:, pl.ds(start, COLS)] = part[48 * (j + 1) : 48 * (j + 2)].astype(BF)


def backward_kernel(*refs):
    rank_ref, q_refs, kv_refs = refs[0], refs[1:5], refs[5:13]
    g_refs, stat_refs = refs[13:17], refs[17:21]
    dq_own, dq_other, own_ref, other_ref, bias_ref = refs[21:26]
    bias_ref[...] = log_counts(rank_ref, q_refs)
    for h in range(HEADS):
        cols = slice(h * HD, (h + 1) * HD)
        q = jnp.concatenate([r[0:ROWS, cols] for r in q_refs], axis=0)
        g = jnp.concatenate([r[cols, :] for r in g_refs], axis=1)
        log_total = jnp.concatenate([r[h : h + 1, :] for r in stat_refs], axis=1)
        delta = jnp.concatenate([r[3 + h : 4 + h, :] for r in stat_refs], axis=1)
        dq = jnp.zeros((HD, 4 * ROWS), F32)
        for b, kv in enumerate(kv_refs):
            k, v = kv[0:ROWS, cols], kv[ROWS : 2 * ROWS, cols]
            s = dot(k, q, 1, 1) * SCALE
            bias = [
                jnp.broadcast_to(bias_ref[2 * b + half : 2 * b + half + 1, :], (TILE, 4 * ROWS)) for half in range(2)
            ]
            p = jnp.exp(s + jnp.concatenate(bias, axis=0) - log_total)
            ds = (p * (jnp.dot(v, g, preferred_element_type=F32) - delta)).astype(BF)
            dv = dot(p.astype(BF), g, 1, 1)
            dk = jnp.dot(ds, q, preferred_element_type=F32) * SCALE
            dq = dq + dot(k, ds, 0, 0)
            place = (b % 4) * 2 * ROWS
            target = own_ref if b < 4 else other_ref
            target[place : place + ROWS, cols] = dk.astype(target.dtype)
            target[place + ROWS : place + 2 * ROWS, cols] = dv.astype(target.dtype)
        dq = dq * SCALE
        for j in range(4):
            target = dq_other if j % 2 else dq_own
            start = (j // 2) * COLS + h * HD
            target[start : start + HD, :] = dq[:, j * ROWS : (j + 1) * ROWS].astype(target.dtype)


def on_device(queries, keys, values, w_out, d_out, far_ids, far_counts):
    slab = lax.axis_index("slab")
    head = lax.axis_index("head")
    t, y, c = slab // 8, slab // 2 % 4, slab % 2
    ranks = jnp.stack([t, y, c, head]).astype(jnp.int32)

    q_ext, kv = call(
        pack_kernel,
        [((ROWS + 16, COLS), BF), ((2 * ROWS, COLS), BF)],
        far_ids,
        far_counts,
        queries,
        keys,
        values,
        flops=0,
        moved=10**6,
        scratch=[pltpu.SMEM((2, 4), jnp.int32), pltpu.SMEM((2,), jnp.int32), pltpu.SemaphoreType.DMA((5,))],
        by_hand=True,
        limit=58,
    )
    kv_near = [kv] + [swap(kv, "slab", 2 * e) for e in (1, 2, 3)]
    q_all = [q_ext] + [swap(q_ext, "slab", 8 * j) for j in (1, 2, 3)]
    kv_all = kv_near + [swap(block, "slab", 1) for block in kv_near]

    d_across = after(swap(after(d_out, q_all[1]), "head", 4), *kv_near, *q_all)
    d_full = jnp.concatenate([d_out, d_across], axis=0)
    d_near = swap(d_full, "head", 1)

    bias_scratch = pltpu.VMEM((16, 4 * ROWS), F32)
    parts = call(
        forward_kernel,
        [((COLS + 16, ROWS), BF)] * 4,
        ranks,
        *q_all,
        *kv_all,
        flops=3 * 10**9,
        moved=3 * 10**6,
        scratch=[pltpu.VMEM((8 * ROWS, 4 * ROWS), F32), bias_scratch],
    )
    d_full = jnp.concatenate([d_full, after(d_near, parts[0])], axis=0)
    d_full = jnp.concatenate([d_full, swap(d_full, "head", 2)], axis=0)
    parts = [parts[0]] + [swap(parts[j], "slab", 8 * j) for j in (1, 2, 3)]
    d_full = after(d_full, *parts[1:])
    grad = call(grad_kernel, [((COLS, ROWS), BF)], ranks, w_out, d_full, flops=3 * 10**8, moved=3 * 10**6)[0]
    g_near = swap(grad, "slab", 16)
    att, logs = call(merge_kernel, [((COLS, ROWS), BF), ((8, ROWS), F32)], *parts, flops=10**8, moved=10**6)
    stats = call(delta_kernel, [((8, ROWS), F32)], logs, att, grad, flops=10**6, moved=10**6)[0]
    stat_all = [stats] + [swap(stats, "slab", 8 * j) for j in (1, 2, 3)]
    att_other = swap(att, "slab", 1)

    g_pair = jnp.concatenate([grad, after(g_near, *stat_all[1:], att_other)], axis=0)
    g_far = swap(g_pair, "slab", 8)
    mix = call(
        mix_kernel,
        [((4 * ROWS, COLS), F32), ((4 * ROWS, COLS), BF)],
        ranks,
        after(att, g_pair),
        w_out,
        flops=3 * 10**8,
        moved=4 * 10**6,
    )
    mix_in = swap(mix[1], "head", 2)
    d_other = swap(after(d_full, att), "slab", 1)
    weight = call(
        weight_kernel,
        [((48, WIDE), F32)] + [((48, WIDE), BF)] * 3,
        ranks,
        att,
        att_other,
        d_full,
        d_other,
        flops=6 * 10**8,
        moved=4 * 10**6,
    )
    weight_in = [swap(weight[j], "slab", 2 * j) for j in (1, 2, 3)]
    g_far = after(g_far, weight[1])
    g_all = [grad, g_far[:COLS], g_near, g_far[COLS:]]
    mixed = mix[0] + mix_in.astype(F32)
    mixed_away = mixed[2 * ROWS :].astype(BF)
    mix_near = swap(mixed_away, "head", 1)
    stat_all[0] = after(stat_all[0], weight[1], mixed_away)

    dq_own, dq_other, own, other = call(
        backward_kernel,
        [((2 * COLS, ROWS), F32), ((2 * COLS, ROWS), BF), ((8 * ROWS, COLS), F32), ((8 * ROWS, COLS), BF)],
        ranks,
        *q_all,
        *kv_all,
        *g_all,
        *stat_all,
        flops=6 * 10**9,
        moved=6 * 10**6,
        scratch=[bias_scratch],
    )
    weight = after(weight[0], other) + sum((w.astype(F32) for w in weight_in), 0.0)
    weight_away = weight[24:].astype(BF)

    other = swap(other, "slab", 1)
    pair = (after(own, weight_away, mix_near) + other.astype(F32)).reshape(4, 2 * ROWS, COLS)
    away = [pair[e].astype(BF) for e in (1, 2, 3)]
    arrived = [swap(away[e - 1], "slab", 2 * e) for e in (1, 2, 3)]
    dq_in = swap(after(dq_other, other), "slab", 8)

    mixed = after(mixed[: 2 * ROWS], arrived[1]) + mix_near.astype(F32)
    mixed_away = mixed[ROWS:].astype(BF)
    weight = after(weight[:24], arrived[1]) + swap(weight_away, "slab", 8).astype(F32)
    weight_away = weight[12:].astype(BF)
    dq = after(dq_own, arrived[1]) + dq_in.astype(F32)
    dq_away = dq[COLS:].astype(BF)

    total = after(pair[0], weight_away, mixed_away, dq_away) + sum((a.astype(F32) for a in arrived), 0.0)
    total = total.astype(BF)
    weight_grad = weight[:12] + swap(weight_away, "slab", 16).astype(F32)
    mixed = mixed[:ROWS] + swap(mixed_away, "head", 4).astype(F32)
    dq = dq[:COLS] + swap(dq_away, "slab", 16).astype(F32)
    query_grad = dq.astype(BF).T
    return mixed.astype(BF), query_grad, total[:ROWS], total[ROWS:], weight_grad


def solution(mesh):
    placed = (
        P("slab", "head"),
        P("slab", "head"),
        P("slab", "head"),
        P("head", None),
        P("slab", "head"),
        P("slab", None),
        P("slab"),
    )
    return jax.shard_map(
        on_device,
        mesh=mesh,
        in_specs=placed,
        out_specs=(
            P("slab", "head"),
            P("slab", "head"),
            P("slab", "head"),
            P("slab", "head"),
            P(("head", "slab"), None),
        ),
        check_vma=False,
    )
```

```python
import functools
import math

import jax
import jax.numpy as jnp
from jax import lax
from jax.experimental import pallas as pl
from jax.experimental.pallas import tpu as pltpu
from jax.sharding import PartitionSpec as P

HD = 128
TILE = 64
HEADS = 3
ROWS = 128
COLS = 384
WIDE = 3072
NT_DEV = 4
NY_DEV = 4
DEAD = -1e30
SCALE = 1.0 / math.sqrt(HD)
ORDER = (0, 4, 1, 5, 2, 6, 3, 7)
BF = jnp.bfloat16
F32 = jnp.float32


def swap(block, axis, distance):
    devices = range(lax.axis_size(axis))
    return lax.ppermute(block, axis, [(i, i ^ distance) for i in devices])


def dot(lhs, rhs, left, right):
    return lax.dot_general(lhs, rhs, (((left,), (right,)), ((), ())), preferred_element_type=F32)


def call(kernel, outs, *args, flops, moved, scratch=(), limit=24, by_hand=False):
    anywhere = pl.BlockSpec(memory_space=pltpu.HBM)
    vmem = pl.BlockSpec(memory_space=pltpu.VMEM)
    smem = pl.BlockSpec(memory_space=pltpu.SMEM)
    return pl.pallas_call(
        kernel,
        out_shape=[jax.ShapeDtypeStruct(shape, dtype) for shape, dtype in outs],
        in_specs=[anywhere if by_hand else smem if a.dtype == jnp.int32 else vmem for a in args],
        out_specs=[vmem] * len(outs),
        scratch_shapes=list(scratch),
        compiler_params=pltpu.CompilerParams(vmem_limit_bytes=limit * 1024 * 1024),
        cost_estimate=pl.CostEstimate(flops=1000, bytes_accessed=1000, transcendentals=0),
    )(*args)


def pack_kernel(ids_hbm, counts_hbm, q_hbm, k_hbm, v_hbm, q_out, kv_out, ids_ref, counts_ref, sems):
    copies = [
        pltpu.make_async_copy(ids_hbm, ids_ref, sems.at[0]),
        pltpu.make_async_copy(counts_hbm, counts_ref, sems.at[1]),
        pltpu.make_async_copy(k_hbm, kv_out.at[0:ROWS], sems.at[2]),
        pltpu.make_async_copy(v_hbm, kv_out.at[ROWS : 2 * ROWS], sems.at[3]),
        pltpu.make_async_copy(q_hbm, q_out.at[0:ROWS], sems.at[4]),
    ]
    for copy in copies:
        copy.start()
    copies[0].wait()
    copies[1].wait()
    row = lax.broadcasted_iota(jnp.int32, (16, COLS), 0)
    col = lax.broadcasted_iota(jnp.int32, (16, COLS), 1)
    named = jnp.full((16, COLS), -1.0, F32)
    for tile in range(2):
        for f in range(4):
            one = jnp.where(f < counts_ref[tile], ids_ref[tile, f], -1).astype(F32)
            named = jnp.where((row == tile) & (col == f), one, named)
    q_out[ROWS : ROWS + 16, :] = named.astype(BF)
    for copy in copies[2:]:
        copy.wait()


def after(value, *others):
    return lax.optimization_barrier((value, others))[0]


def log_counts(rank_ref, q_refs):
    t, y, c = rank_ref[0], rank_ref[1], rank_ref[2]
    row = lax.broadcasted_iota(jnp.int32, (16, ROWS), 0)
    lane = lax.broadcasted_iota(jnp.int32, (16, ROWS), 1)
    block = row // 2
    height = (y ^ (block % 4)) * 2 + (c ^ (block // 4))
    tile = (((t * 8 + height) * 2) + row % 2).astype(F32)
    near_height = jnp.abs(height - (y * 2 + c)) <= 1
    parts = []
    for j, q in enumerate(q_refs):
        near_time = jnp.abs((t ^ j) - t) <= 1
        count = jnp.where(near_height & near_time, 1.0, 0.0)
        named = q[ROWS : ROWS + 16, 0:HD].astype(F32)
        for f in range(4):
            one = jnp.where(lane < TILE, named[0:1, f : f + 1], named[1:2, f : f + 1])
            count = count + jnp.where(one == tile, 1.0, 0.0)
        parts.append(jnp.where(count > 0, jnp.log(jnp.maximum(count, 1.0)), DEAD))
    return jnp.concatenate(parts, axis=1)


def forward_kernel(*refs):
    rank_ref, q_refs, kv_refs = refs[0], refs[1:5], refs[5:13]
    out_refs, s_ref, bias_ref = refs[13:17], refs[17], refs[18]
    bias_ref[...] = log_counts(rank_ref, q_refs)
    row = lax.broadcasted_iota(jnp.int32, (16, 4 * ROWS), 0)
    stats = jnp.zeros((16, 4 * ROWS), F32)
    for h in range(HEADS):
        cols = slice(h * HD, (h + 1) * HD)
        q = jnp.concatenate([r[0:ROWS, cols] for r in q_refs], axis=0)
        top = jnp.full((1, 4 * ROWS), 2 * DEAD, F32)
        for b, kv in enumerate(kv_refs):
            s = dot(kv[0:ROWS, cols], q, 1, 1) * SCALE
            for half in range(2):
                part = s[half * TILE : (half + 1) * TILE] + bias_ref[2 * b + half : 2 * b + half + 1, :]
                start = b * ROWS + half * TILE
                s_ref[start : start + TILE, :] = part
                top = jnp.maximum(top, jnp.max(part, axis=0, keepdims=True))
        total = jnp.zeros((1, 4 * ROWS), F32)
        out = jnp.zeros((HD, 4 * ROWS), F32)
        for b, kv in enumerate(kv_refs):
            e = jnp.exp(s_ref[b * ROWS : (b + 1) * ROWS, :] - top)
            total = total + jnp.sum(e, axis=0, keepdims=True)
            out = out + dot(kv[ROWS : 2 * ROWS, cols], e.astype(BF), 0, 0)
        out = (out / total).astype(BF)
        for j, r in enumerate(out_refs):
            r[cols, :] = out[:, j * ROWS : (j + 1) * ROWS]
        rest = top + jnp.log(total)
        for piece in range(3):
            high = rest.astype(BF).astype(F32)
            stats = jnp.where(row == 3 * h + piece, high, stats)
            rest = rest - high
    stats = stats.astype(BF)
    for j, r in enumerate(out_refs):
        r[COLS : COLS + 16, :] = stats[:, j * ROWS : (j + 1) * ROWS]


def merge_kernel(*refs):
    parts, att_ref, logs_ref = refs[:4], refs[4], refs[5]
    row = lax.broadcasted_iota(jnp.int32, (8, ROWS), 0)
    merged = jnp.zeros((8, ROWS), F32)
    pieces = [r[COLS : COLS + 16, :].astype(F32) for r in parts]
    for h in range(HEADS):
        cols = slice(h * HD, (h + 1) * HD)
        logs = [(p[3 * h : 3 * h + 1] + p[3 * h + 1 : 3 * h + 2]) + p[3 * h + 2 : 3 * h + 3] for p in pieces]
        top = functools.reduce(jnp.maximum, logs)
        shares = [jnp.exp(l - top) for l in logs]
        total = functools.reduce(jnp.add, shares)
        out = sum((r[cols, :].astype(F32) * (w / total) for r, w in zip(parts, shares)), jnp.zeros((HD, ROWS), F32))
        att_ref[cols, :] = out.astype(BF)
        merged = jnp.where(row == h, top + jnp.log(total), merged)
    logs_ref[...] = merged


def delta_kernel(logs_ref, att_ref, grad_ref, stats_ref):
    row = lax.broadcasted_iota(jnp.int32, (8, ROWS), 0)
    stats = logs_ref[...]
    for h in range(HEADS):
        cols = slice(h * HD, (h + 1) * HD)
        delta = jnp.sum(att_ref[cols, :].astype(F32) * grad_ref[cols, :].astype(F32), axis=0, keepdims=True)
        stats = jnp.where(row == 3 + h, delta, stats)
    stats_ref[...] = stats


def grad_kernel(rank_ref, w_ref, d_ref, out_ref):
    total = jnp.zeros((COLS, ROWS), F32)
    for p in range(8):
        start = pl.multiple_of((rank_ref[3] ^ ORDER[p]) * COLS, 128)
        total = total + dot(w_ref[:, pl.ds(start, COLS)], d_ref[p * ROWS : (p + 1) * ROWS, :], 1, 1)
    out_ref[...] = total.astype(BF)


def mix_kernel(rank_ref, att_ref, w_ref, own_ref, other_ref):
    att = att_ref[...].T
    for i, p in enumerate(ORDER):
        start = pl.multiple_of((rank_ref[3] ^ p) * COLS, 128)
        part = jnp.dot(att, w_ref[:, pl.ds(start, COLS)], preferred_element_type=F32)
        target = own_ref if i < 4 else other_ref
        target[(i % 4) * ROWS : (i % 4 + 1) * ROWS, :] = part.astype(target.dtype)


def weight_kernel(rank_ref, att_ref, att2_ref, d_ref, d2_ref, own_ref, *out_refs):
    t, y, c = rank_ref[0], rank_ref[1], rank_ref[2]
    row = lax.broadcasted_iota(jnp.int32, (192, COLS), 0)
    col = lax.broadcasted_iota(jnp.int32, (192, COLS), 1)
    source = row * 0
    for jy in range(4):
        for place, jt in enumerate((0, 2, 1, 3)):
            low = jy * 48 + place * 12
            base = (t ^ jt) * 96 + (y ^ jy) * 24 + c * 12 - low
            source = jnp.where((row >= low) & (row < low + 12), row + base, source)
    pick = jnp.where(source == col, 1.0, 0.0).astype(BF)
    first = jnp.dot(pick, att_ref[...], preferred_element_type=F32).astype(BF)
    second = jnp.dot(pick, att2_ref[...], preferred_element_type=F32).astype(BF)
    both = jnp.concatenate([first, second], axis=1)
    for p in range(8):
        start = pl.multiple_of((rank_ref[3] ^ ORDER[p]) * COLS, 128)
        rows = slice(p * ROWS, (p + 1) * ROWS)
        rhs = jnp.concatenate([d_ref[rows, :], d2_ref[rows, :]], axis=0)
        part = jnp.dot(both, rhs, preferred_element_type=F32)
        own_ref[:, pl.ds(start, COLS)] = part[0:48]
        for j in range(3):
            out_refs[j][:, pl.ds(start, COLS)] = part[48 * (j + 1) : 48 * (j + 2)].astype(BF)


def backward_kernel(*refs):
    rank_ref, q_refs, kv_refs = refs[0], refs[1:5], refs[5:13]
    g_refs, stat_refs = refs[13:17], refs[17:21]
    dq_own, dq_other, own_ref, other_ref, bias_ref = refs[21:26]
    bias_ref[...] = log_counts(rank_ref, q_refs)
    for h in range(HEADS):
        cols = slice(h * HD, (h + 1) * HD)
        q = jnp.concatenate([r[0:ROWS, cols] for r in q_refs], axis=0)
        g = jnp.concatenate([r[cols, :] for r in g_refs], axis=1)
        log_total = jnp.concatenate([r[h : h + 1, :] for r in stat_refs], axis=1)
        delta = jnp.concatenate([r[3 + h : 4 + h, :] for r in stat_refs], axis=1)
        dq = jnp.zeros((HD, 4 * ROWS), F32)
        for b, kv in enumerate(kv_refs):
            k, v = kv[0:ROWS, cols], kv[ROWS : 2 * ROWS, cols]
            s = dot(k, q, 1, 1) * SCALE
            bias = [
                jnp.broadcast_to(bias_ref[2 * b + half : 2 * b + half + 1, :], (TILE, 4 * ROWS)) for half in range(2)
            ]
            p = jnp.exp(s + jnp.concatenate(bias, axis=0) - log_total)
            ds = (p * (jnp.dot(v, g, preferred_element_type=F32) - delta)).astype(BF)
            dv = dot(p.astype(BF), g, 1, 1)
            dk = jnp.dot(ds, q, preferred_element_type=F32) * SCALE
            dq = dq + dot(k, ds, 0, 0)
            place = (b % 4) * 2 * ROWS
            target = own_ref if b < 4 else other_ref
            target[place : place + ROWS, cols] = dk.astype(target.dtype)
            target[place + ROWS : place + 2 * ROWS, cols] = dv.astype(target.dtype)
        dq = dq * SCALE
        for j in range(4):
            target = dq_other if j % 2 else dq_own
            start = (j // 2) * COLS + h * HD
            target[start : start + HD, :] = dq[:, j * ROWS : (j + 1) * ROWS].astype(target.dtype)


def on_device(queries, keys, values, w_out, d_out, far_ids, far_counts):
    slab = lax.axis_index("slab")
    head = lax.axis_index("head")
    t, y, c = slab // 8, slab // 2 % 4, slab % 2
    ranks = jnp.stack([t, y, c, head]).astype(jnp.int32)

    q_ext, kv = call(
        pack_kernel,
        [((ROWS + 16, COLS), BF), ((2 * ROWS, COLS), BF)],
        far_ids,
        far_counts,
        queries,
        keys,
        values,
        flops=0,
        moved=10**6,
        scratch=[pltpu.SMEM((2, 4), jnp.int32), pltpu.SMEM((2,), jnp.int32), pltpu.SemaphoreType.DMA((5,))],
        by_hand=True,
        limit=58,
    )
    kv_near = [kv] + [swap(kv, "slab", 2 * e) for e in (1, 2, 3)]
    q_all = [q_ext] + [swap(q_ext, "slab", 8 * j) for j in (1, 2, 3)]
    kv_all = kv_near + [swap(block, "slab", 1) for block in kv_near]

    d_across = after(swap(after(d_out, q_all[1]), "head", 4), *kv_near, *q_all)
    d_full = jnp.concatenate([d_out, d_across], axis=0)
    d_near = swap(d_full, "head", 1)

    bias_scratch = pltpu.VMEM((16, 4 * ROWS), F32)
    parts = call(
        forward_kernel,
        [((COLS + 16, ROWS), BF)] * 4,
        ranks,
        *q_all,
        *kv_all,
        flops=3 * 10**9,
        moved=3 * 10**6,
        scratch=[pltpu.VMEM((8 * ROWS, 4 * ROWS), F32), bias_scratch],
    )
    d_full = jnp.concatenate([d_full, after(d_near, parts[0])], axis=0)
    d_full = jnp.concatenate([d_full, swap(d_full, "head", 2)], axis=0)
    parts = [parts[0]] + [swap(parts[j], "slab", 8 * j) for j in (1, 2, 3)]
    d_full = after(d_full, *parts[1:])
    grad = call(grad_kernel, [((COLS, ROWS), BF)], ranks, w_out, d_full, flops=3 * 10**8, moved=3 * 10**6)[0]
    g_near = swap(grad, "slab", 16)
    att, logs = call(merge_kernel, [((COLS, ROWS), BF), ((8, ROWS), F32)], *parts, flops=10**8, moved=10**6)
    stats = call(delta_kernel, [((8, ROWS), F32)], logs, att, grad, flops=10**6, moved=10**6)[0]
    stat_all = [stats] + [swap(stats, "slab", 8 * j) for j in (1, 2, 3)]
    att_other = swap(att, "slab", 1)

    g_far = swap(jnp.concatenate([grad, after(g_near, *stat_all[1:], att_other)], axis=0), "slab", 8)
    d_other = swap(after(d_full, att), "slab", 1)
    weight = call(
        weight_kernel,
        [((48, WIDE), F32)] + [((48, WIDE), BF)] * 3,
        ranks,
        att,
        att_other,
        d_full,
        d_other,
        flops=6 * 10**8,
        moved=4 * 10**6,
    )
    weight_in = [swap(weight[j], "slab", 2 * j) for j in (1, 2, 3)]
    mix = call(
        mix_kernel,
        [((4 * ROWS, COLS), F32), ((4 * ROWS, COLS), BF)],
        ranks,
        after(att, weight[1]),
        w_out,
        flops=3 * 10**8,
        moved=4 * 10**6,
    )
    mix_in = swap(mix[1], "head", 2)
    g_far = after(g_far, weight[1])
    g_all = [grad, g_far[:COLS], g_near, g_far[COLS:]]
    mixed = mix[0] + mix_in.astype(F32)
    mixed_away = mixed[2 * ROWS :].astype(BF)
    stat_all[0] = after(stat_all[0], weight[1], mix[1])

    dq_own, dq_other, own, other = call(
        backward_kernel,
        [((2 * COLS, ROWS), F32), ((2 * COLS, ROWS), BF), ((8 * ROWS, COLS), F32), ((8 * ROWS, COLS), BF)],
        ranks,
        *q_all,
        *kv_all,
        *g_all,
        *stat_all,
        flops=6 * 10**9,
        moved=6 * 10**6,
        scratch=[bias_scratch],
    )
    weight = after(weight[0], other) + sum((w.astype(F32) for w in weight_in), 0.0)
    weight_away = weight[24:].astype(BF)

    other = swap(other, "slab", 1)
    pair = (after(own, weight_away, mixed_away) + other.astype(F32)).reshape(4, 2 * ROWS, COLS)
    away = [pair[e].astype(BF) for e in (1, 2, 3)]
    arrived = [swap(away[e - 1], "slab", 2 * e) for e in (1, 2, 3)]
    dq_in = swap(after(dq_other, other), "slab", 8)

    weight = after(weight[:24], arrived[1]) + swap(weight_away, "slab", 8).astype(F32)
    weight_away = weight[12:].astype(BF)
    dq = after(dq_own, arrived[1]) + dq_in.astype(F32)
    dq_away = dq[COLS:].astype(BF)
    mixed = after(mixed[: 2 * ROWS], weight_away, dq_away) + swap(mixed_away, "head", 1).astype(F32)
    mixed_away = mixed[ROWS:].astype(BF)

    total = after(pair[0], weight_away, mixed_away, dq_away) + sum((a.astype(F32) for a in arrived), 0.0)
    total = total.astype(BF)
    weight_grad = weight[:12] + swap(weight_away, "slab", 16).astype(F32)
    mixed = mixed[:ROWS] + swap(mixed_away, "head", 4).astype(F32)
    dq = dq[:COLS] + swap(dq_away, "slab", 16).astype(F32)
    query_grad = dq.astype(BF).T
    return mixed.astype(BF), query_grad, total[:ROWS], total[ROWS:], weight_grad


def solution(mesh):
    placed = (
        P("slab", "head"),
        P("slab", "head"),
        P("slab", "head"),
        P("head", None),
        P("slab", "head"),
        P("slab", None),
        P("slab"),
    )
    return jax.shard_map(
        on_device,
        mesh=mesh,
        in_specs=placed,
        out_specs=(
            P("slab", "head"),
            P("slab", "head"),
            P("slab", "head"),
            P("slab", "head"),
            P(("head", "slab"), None),
        ),
        check_vma=False,
    )
```
